256 devices in a mesh: grp: 2 (over z_hi), az: 64 (over x, z_lo, y), ax: 2 (over core).
Axes of the slice: x: 4, y: 4, z: 8 (z_hi: 2, z_lo: 4; z = z_hi * 4 + z_lo), core: 2. Of those that a mesh axis runs over, the one named last changes fastest.
Arguments:
- cavity_block: float32 [8, 96, 256, 256], P(None, 'grp', 'az', 'ax'), may hold values from -95 to 95
- shell_block: float32 [8, 6, 256, 256], P(None, None, 'az', 'ax'), may hold values from -95 to 95
- column_matrix: float32 [2, 48, 48], P('grp'), may hold values from -2 to 6, as said below
- shell_matrix: float32 [6, 6], replicated, may hold values from -2 to 6, as said below
- shifted_diagonal: float32 [96, 256, 256], P('grp', 'az', 'ax'), may hold values from 1.6 to 3
- shell_diagonal: float32 [6, 256, 256], P(None, 'az', 'ax'), may hold values from 1.6 to 3
- wet_area: float32 [256, 256], P('az', 'ax'), may hold values from 0.3 to 1.5
Outputs:
- cavity_solution: float32 [8, 96, 256, 256], P(None, 'grp', 'az', 'ax')
- cavity_residual: float32 [8, 96, 256, 256], P(None, 'grp', 'az', 'ax')
- shell_solution: float32 [8, 6, 256, 256], P(None, None, 'az', 'ax')
- shell_residual: float32 [8, 6, 256, 256], P(None, None, 'az', 'ax')
The draws below stay inside these ranges and needn't reach their ends.
Inputs may be any that keep to these rules, and one draw needn't show every extreme that they name: `column_matrix`: each symmetric and positive definite. `shell_matrix`: symmetric and positive definite.
All inputs are finite; a program needn't handle non-finite values.
Results may differ from the reference program's by a relative error of at most 0.0015.
Values sent between devices are 32-bit elements; how exact they have to be, the bound alone decides.
A program may use at most 128 MiB of HBM per device.

```python
import math
import jax
import jax.numpy as jnp
from jax import lax

R = 96
RS = 6
NV = 8
ITERS = 3
NA = 256
NX = 256


def block_draw(key, rows):
    normals = jax.random.normal(jax.random.fold_in(key, 11), (NV, rows, NA, NX), jnp.float32)
    normals = jnp.clip(normals, -6.0, 6.0)
    azimuth_scale = 0.5 * 10.0 ** (jnp.arange(NA, dtype=jnp.float32) / NA)
    vector_scale = 10.0 ** (jnp.arange(NV, dtype=jnp.float32) / (NV - 1) - 0.5)
    return normals * azimuth_scale[:, None] * vector_scale[:, None, None, None]


def column_draw(key, count, rows):
    entries = jax.random.normal(jax.random.fold_in(key, 21), (count, rows, rows), jnp.float32)
    mirrored = (entries + jnp.swapaxes(entries, 1, 2)) * (1.8 / rows)
    identity = jnp.eye(rows, dtype=jnp.float32)
    outside = mirrored * (1.0 - identity)
    surplus = jax.random.uniform(jax.random.fold_in(key, 22), (count, rows), jnp.float32, 0.2, 1.0)
    leading = jnp.sum(jnp.abs(outside), axis=2) + surplus
    return outside + identity * leading[:, :, None]


def draw_cavity_block(key, part):
    return block_draw(jax.random.fold_in(key, 1), R)


def draw_shell_block(key, part):
    return block_draw(jax.random.fold_in(key, 2), RS)


def draw_column_matrix(key, part):
    return column_draw(jax.random.fold_in(key, 3), 2, R // 2)


def draw_shell_matrix(key, part):
    return column_draw(jax.random.fold_in(key, 4), 1, RS)[0]


def block_scale(stream_key, extent, split, low, high):
    loudness = 1.0
    for axis_at, parts in split:
        heights = jax.random.uniform(jax.random.fold_in(jax.random.fold_in(stream_key, 6), axis_at), (parts,), jnp.float32, low / len(split), high / len(split))
        loudness = loudness * jnp.repeat(jnp.exp(heights), extent[axis_at] // parts).reshape((-1,) + (1,) * (len(extent) - 1 - axis_at))
    return loudness


def setup_inputs(seed: int = 0) -> dict:
    keys = jax.random.split(jax.random.key(seed), 8)
    cavity_block = draw_cavity_block(jax.random.fold_in(keys[7], 71), 0)
    shell_block = draw_shell_block(jax.random.fold_in(keys[7], 71), 0)
    column_matrix = draw_column_matrix(jax.random.fold_in(keys[7], 71), 0)
    shell_matrix = draw_shell_matrix(jax.random.fold_in(keys[7], 71), 0)
    shifted_diagonal = jnp.clip(1.6 + 1.4 * jax.random.uniform(keys[4], (R, NA, NX), jnp.float32) ** block_scale(keys[4], (R, NA, NX), ((0, 2), (1, 64), (2, 2)), -0.2, 0.2), 1.6, 3.0)
    shell_diagonal = jnp.clip(1.6 + 1.4 * jax.random.uniform(keys[5], (RS, NA, NX), jnp.float32) ** block_scale(keys[5], (RS, NA, NX), ((1, 64), (2, 2)), -0.2, 0.2), 1.6, 3.0)
    wet_area = jnp.clip(jnp.exp(math.log(1.5) - 1.60943787 * jax.random.uniform(keys[6], (NA, NX), jnp.float32) ** block_scale(keys[6], (NA, NX), ((0, 64), (1, 2)), -0.2, 0.2)), 0.3, 1.5)
    return {"cavity_block": cavity_block, "shell_block": shell_block, "column_matrix": column_matrix, "shell_matrix": shell_matrix, "shifted_diagonal": shifted_diagonal, "shell_diagonal": shell_diagonal, "wet_area": wet_area}


exact_mode = lax.Precision.HIGHEST

def solve_posdef(gram_matrix, targets):
    factor = jnp.linalg.cholesky(gram_matrix)
    middle = lax.linalg.triangular_solve(factor, targets, left_side=True, lower=True)
    return lax.linalg.triangular_solve(factor, middle, left_side=True, lower=True, transpose_a=True)

def moments(first_pair, second_pair):
    cavity_part = jnp.einsum('vrax,wrax->vw', first_pair[0], second_pair[0], precision=exact_mode)
    shell_part = jnp.einsum('vrax,wrax->vw', first_pair[1], second_pair[1], precision=exact_mode)
    return cavity_part + shell_part

def combine(vector_pair, mixing):
    return (jnp.einsum('vrax,vw->wrax', vector_pair[0], mixing, precision=exact_mode), jnp.einsum('vrax,vw->wrax', vector_pair[1], mixing, precision=exact_mode))

def stencil(field, diagonal):
    padded = jnp.pad(field, ((0, 0), (0, 0), (0, 0), (1, 1)))
    neighbours = jnp.roll(field, 1, axis=2) + jnp.roll(field, -1, axis=2)
    neighbours = neighbours + padded[..., 2:] + padded[..., :-2]
    return (4.0 + diagonal[None]) * field - neighbours

def operate(vector_pair, column_matrix, shell_matrix, shifted_diagonal, shell_diagonal, wet_area):
    cavity, shell = vector_pair
    half = R // 2
    inner = jnp.einsum('rs,vsax->vrax', column_matrix[0], cavity[:, :half], precision=exact_mode)
    outer = jnp.einsum('rs,vsax->vrax', column_matrix[1], cavity[:, half:], precision=exact_mode)
    cavity_out = jnp.concatenate([inner, outer], axis=1) + stencil(cavity, shifted_diagonal)
    cavity_out = cavity_out.at[:, half - 1].add(-cavity[:, half])
    cavity_out = cavity_out.at[:, half].add(-cavity[:, half - 1])
    cavity_out = cavity_out.at[:, R - 1].add(-wet_area * shell[:, 0])
    shell_out = jnp.einsum('rs,vsax->vrax', shell_matrix, shell, precision=exact_mode) + stencil(shell, shell_diagonal)
    shell_out = shell_out.at[:, 0].add(-wet_area * cavity[:, R - 1])
    return (cavity_out, shell_out)

def reference(cavity_block, shell_block, column_matrix, shell_matrix, shifted_diagonal, shell_diagonal, wet_area):
    residual = (cavity_block, shell_block)
    direction = residual
    solution = (jnp.zeros_like(cavity_block), jnp.zeros_like(shell_block))
    norms_now = moments(residual, residual)
    for sweep in range(ITERS):
        image_set = operate(direction, column_matrix, shell_matrix, shifted_diagonal, shell_diagonal, wet_area)
        step_mix = solve_posdef(moments(direction, image_set), norms_now)
        moved = combine(direction, step_mix)
        solution = (solution[0] + moved[0], solution[1] + moved[1])
        pulled = combine(image_set, step_mix)
        residual = (residual[0] - pulled[0], residual[1] - pulled[1])
        if sweep + 1 < ITERS:
            norms_next = moments(residual, residual)
            turn_mix = solve_posdef(norms_now, norms_next)
            turned = combine(direction, turn_mix)
            direction = (residual[0] + turned[0], residual[1] + turned[1])
            norms_now = norms_next
    return (solution[0], residual[0], solution[1], residual[1])
```

```python
import jax
import jax.numpy as jnp
from jax import lax
from jax.experimental import pallas as pl
from jax.experimental.pallas import tpu as pltpu
from jax.sharding import PartitionSpec as P

NV = 8
RC = 48
RS = 6
ROWS = 56
AZL = 4
BLK = AZL * ROWS
STEPS = 3
THETA = 9.0
MESH = pl.DeviceIdType.MESH
F32 = jnp.float32
BF16 = jnp.bfloat16


def rounded(value):
    return value.astype(BF16).astype(F32)


def kernel(
    cav, shl, colm, shm, dia, sdia, wet,
    sol_c, res_c, sol_s, res_s,
    X, HL, HR, SB, IS, IR, DG, W, STG, ACC, RX1, RX2,
    raw_c, raw_s, raw_d, raw_sd, raw_w, raw_cm, raw_sm,
    o_sc, o_rc, o_ss, o_rs,
    in_sem, out_sem, send_sem, recv_sem, s1, r1, s2, r2,
):
    grp = lax.axis_index("grp")
    az = lax.axis_index("az")
    ax = lax.axis_index("ax")
    naz = 64
    right = lax.rem(az + 1, naz)
    left = lax.rem(az + naz - 1, naz)
    px = az // 16
    pz = lax.rem(az // 4, 4)
    py = lax.rem(az, 4)

    loads = [
        pltpu.make_async_copy(src, dst, in_sem.at[i])
        for i, (src, dst) in enumerate(
            [(cav, raw_c), (shl, raw_s), (dia, raw_d), (sdia, raw_sd), (wet, raw_w), (colm, raw_cm), (shm, raw_sm)]
        )
    ]
    for load in loads:
        load.start()

    barrier = pltpu.get_barrier_semaphore()

    def hello(where):
        pl.semaphore_signal(barrier, inc=1, device_id=where, device_id_type=MESH)

    me1 = px * 4 + py
    me2 = grp * 8 + pz * 2 + ax

    def peer1(d):
        s = lax.rem(me1 + d, 16)
        return s, {"grp": grp, "az": (s // 4) * 16 + pz * 4 + lax.rem(s, 4), "ax": ax}

    def peer2(d):
        s = lax.rem(me2 + d, 16)
        return s, {"grp": s // 8, "az": px * 16 + lax.rem(s // 2, 4) * 4 + py, "ax": lax.rem(s, 2)}

    to_right = {"grp": grp, "az": right, "ax": ax}
    to_left = {"grp": grp, "az": left, "ax": ax}
    to_core = {"grp": grp, "az": az, "ax": 1 - ax}
    to_half = {"grp": 1 - grp, "az": az, "ax": ax}
    for where in (to_right, to_left, to_core, to_half):
        hello(where)

    def hello_peers(d, c):
        hello(peer1(d)[1])
        hello(peer2(d)[1])
        return c

    lax.fori_loop(1, 16, hello_peers, 0)

    outer = (grp == 1).astype(F32)
    is_outer = grp == 1
    lane = lax.broadcasted_iota(jnp.int32, (8, 128), 1)
    row = lax.broadcasted_iota(jnp.int32, (8, 128), 0)

    for load in loads:
        load.wait()

    def place(v, c):
        for a in range(AZL):
            at = v * BLK + a * ROWS
            X[0, pl.ds(pl.multiple_of(at, 8), RC), :] = raw_c[pl.ds(v * (RC * AZL) + a, RC, stride=AZL), :]
            tail = jnp.concatenate(
                [raw_s[pl.ds(v * (RS * AZL) + a, RS, stride=AZL), :], jnp.zeros((2, 128), F32)], axis=0
            )
            X[0, pl.ds(pl.multiple_of(at + RC, 8), 8), :] = tail
        return c

    lax.fori_loop(0, NV, place, 0)

    def rows_to_send(k, v):
        for a in range(AZL):
            at = v * BLK + a * ROWS
            first = X[k, pl.ds(pl.multiple_of(at, 8), 8), :][0:1]
            last = X[k, pl.ds(pl.multiple_of(at + 40, 8), 8), :][7:8]
            IS[k, v, a : a + 1, :] = jnp.where(is_outer, first, last)
            IS[k, v, 4 + a : 5 + a, :] = last

    def exchange(k, v):
        base = pl.multiple_of(v * BLK, 8)
        top = pl.multiple_of(v * BLK + 3 * ROWS, 8)
        return (
            pltpu.make_async_remote_copy(
                X.at[k, pl.ds(top, ROWS), :], HL.at[k, v], send_sem.at[k, 0], recv_sem.at[k, v, 0],
                device_id=to_right, device_id_type=MESH,
            ),
            pltpu.make_async_remote_copy(
                X.at[k, pl.ds(base, ROWS), :], HR.at[k, v], send_sem.at[k, 1], recv_sem.at[k, v, 1],
                device_id=to_left, device_id_type=MESH,
            ),
            pltpu.make_async_remote_copy(
                X.at[k, pl.ds(base, BLK), :], SB.at[k, v], send_sem.at[k, 2], recv_sem.at[k, v, 2],
                device_id=to_core, device_id_type=MESH,
            ),
            pltpu.make_async_remote_copy(
                IS.at[k, v], IR.at[k, v], send_sem.at[k, 3], recv_sem.at[k, v, 3],
                device_id=to_half, device_id_type=MESH,
            ),
        )

    def sent(k):
        for i, (buf, where) in enumerate(((HL, to_right), (HR, to_left), (SB, to_core), (IS, to_half))):
            pltpu.make_async_remote_copy(
                buf.at[k], buf.at[k], send_sem.at[k, i], recv_sem.at[k, 0, i], device_id=where, device_id_type=MESH
            ).wait_send()

    pl.semaphore_wait(barrier, 34)

    def first_send(v, c):
        rows_to_send(0, v)
        for copy in exchange(0, v):
            copy.start()
        return c

    lax.fori_loop(0, NV, first_send, 0)

    for a in range(AZL):
        DG[a, 0:RC, :] = raw_d[pl.ds(a, RC, stride=AZL), :] + (4.0 - THETA)
        DG[a, RC:ROWS, :] = jnp.concatenate(
            [raw_sd[pl.ds(a, RS, stride=AZL), :] + (4.0 - THETA), jnp.zeros((2, 128), F32)], axis=0
        )
    STG[...] = jnp.zeros((64, 128), F32)
    STG[56:62, 0:RS] = raw_sm[...]
    shell_rows = pltpu.roll(STG[56:64, :], RC, axis=1)
    STG[56:64, :] = jnp.zeros((8, 128), F32)
    STG[0:RC, 0:RC] = raw_cm[...]
    STG[RC:ROWS, :] = shell_rows
    row64 = lax.broadcasted_iota(jnp.int32, (64, 128), 0)
    lane64 = lax.broadcasted_iota(jnp.int32, (64, 128), 1)
    iface = jnp.where(is_outer, 0, RC - 1)
    matrix = STG[...]
    matrix = jnp.where((lane64 == 56) & (row64 == iface), -1.0, matrix)
    matrix = jnp.where((lane64 == 57) & (row64 == RC), -1.0, matrix)
    matrix = jnp.where((lane64 == 58) & (row64 == RC - 1), -outer, matrix)
    high = rounded(matrix)
    W[...] = jnp.concatenate([high + pltpu.roll(high, 64, axis=1), matrix - high], axis=1).astype(BF16)

    lane56 = lax.broadcasted_iota(jnp.int32, (ROWS, 128), 1)
    first_lane = lane56 == 0
    last_lane = lane56 == 127
    from_left = (ax == 1).astype(F32)
    from_right = (ax == 0).astype(F32)
    share = 1.0 - outer

    def apply(k):
        def body(v, moments):
            base = v * BLK
            for copy in exchange(k, v):
                copy.wait_recv()
            own = [X[k, pl.ds(pl.multiple_of(base + a * ROWS, 8), ROWS), :] for a in range(AZL)]
            got = IR[k, v]
            spread = []
            for a in range(AZL):
                wet_row = raw_w[a : a + 1, :]
                wall = jnp.where(is_outer, own[a][RC - 1 : RC], got[4 + a : 5 + a])
                skin = own[a][RC : RC + 1]
                extra = jnp.where(row == 0, got[a : a + 1], 0.0)
                extra = jnp.where(row == 1, wet_row * wall, extra)
                extra = jnp.where(row == 2, wet_row * skin, extra)
                spread.append(jnp.concatenate([own[a], extra], axis=0))
            wide = jnp.concatenate(spread, axis=1)
            high = rounded(wide)
            stacked = jnp.concatenate([high, wide - high, high], axis=0).astype(BF16)
            mixed = jnp.dot(W[:, 0:192], stacked, preferred_element_type=F32)
            for a in range(AZL):
                side = SB[k, v, a * ROWS : (a + 1) * ROWS, :]
                before = HL[k, v] if a == 0 else own[a - 1]
                after = HR[k, v] if a == AZL - 1 else own[a + 1]
                lower = pltpu.roll(jnp.where(last_lane, side * from_left, own[a]), 1, axis=1)
                upper = pltpu.roll(jnp.where(first_lane, side * from_right, own[a]), 127, axis=1)
                new = mixed[0:ROWS, a * 128 : (a + 1) * 128] + DG[a] * own[a]
                new = new - ((before + after) + (lower + upper))
                X[k + 1, pl.ds(pl.multiple_of(base + a * ROWS, 8), ROWS), :] = new
            if k + 1 < STEPS:
                rows_to_send(k + 1, v)
                for copy in exchange(k + 1, v):
                    copy.start()
            even = [jnp.zeros((8, 128), F32) for _ in range(NV)]
            odd = [jnp.zeros((8, 128), F32) for _ in range(NV)]
            for p in range(BLK // 8):
                here = pl.ds(pl.multiple_of(base + p * 8, 8), 8)
                old, new = X[k, here, :], X[k + 1, here, :]
                if p % 7 == 6:
                    old, new = old * share, new * share
                for w in range(NV):
                    other = X[k, w * BLK + p * 8 : w * BLK + p * 8 + 8, :]
                    even[w] += other * old
                    odd[w] += other * new
            for w in range(NV):
                ACC[w * 8 : w * 8 + 8, :] = even[w]
                ACC[64 + w * 8 : 72 + w * 8, :] = odd[w]
            for half in range(2):
                total = ACC[pl.ds(64 * half, 8, stride=8), :]
                for s in range(1, 8):
                    total += ACC[pl.ds(64 * half + s, 8, stride=8), :]
                total = jnp.sum(total, axis=1, keepdims=True)
                moments = jnp.where(lane == 8 * (2 * k + half) + v, total, moments)
            return moments

        return body

    moments = jnp.zeros((8, 128), F32)
    for k in range(STEPS):
        moments = lax.fori_loop(0, NV, apply(k), moments)

    def total_of(value, me, peer, buf, ssem, rsem):
        buf[me] = value

        def copy_of(d):
            s, where = peer(d)
            return s, pltpu.make_async_remote_copy(
                buf.at[me], buf.at[me], ssem.at[d], rsem.at[me], device_id=where, device_id_type=MESH
            )

        def start(d, c):
            copy_of(d)[1].start()
            return c

        def wait(d, c):
            s, where = peer(d)
            pltpu.make_async_remote_copy(
                buf.at[s], buf.at[s], ssem.at[d], rsem.at[s], device_id=where, device_id_type=MESH
            ).wait_recv()
            return c

        def drain(d, c):
            copy_of(d)[1].wait_send()
            return c

        lax.fori_loop(1, 16, start, 0)
        lax.fori_loop(1, 16, wait, 0)
        result = buf[0]
        for s in range(1, 16):
            result += buf[s]
        lax.fori_loop(1, 16, drain, 0)
        return result

    gram = total_of(moments, me1, peer1, RX1, s1, r1)
    gram = total_of(gram, me2, peer2, RX2, s2, r2)

    shifted = pltpu.roll(gram, 120, axis=1) + THETA * gram
    table = []
    for i in range(STEPS):
        left_part = shifted if i == 0 else pltpu.roll(shifted, 128 - 8 * i, axis=1)
        right_part = pltpu.roll(gram, 24 - 8 * i, axis=1)
        table.append(jnp.where(lane < 24, left_part, jnp.where(lane < 32, right_part, 0.0)))
    for p in range(8 * STEPS):
        at, r = p // 8, p % 8
        pivot_row = table[at][r : r + 1, :]
        scaled = pivot_row * (1.0 / pivot_row[:, p : p + 1])
        for i in range(STEPS):
            column = table[i][:, p : p + 1]
            reduced = table[i] - column * scaled
            table[i] = jnp.where(row == r, scaled, reduced) if i == at else reduced

    y = [jnp.where(lane < 8, pltpu.roll(t, 104, axis=1), 0.0) for t in table]
    eye = jnp.where(lane == row, 1.0, 0.0)
    into = [
        eye - THETA * y[0],
        -(y[0] + THETA * y[1]),
        -(y[1] + THETA * y[2]),
        -y[2],
    ]
    zero8 = jnp.zeros((8, 128), F32)
    parts = [(y[k] if k < STEPS else zero8) + pltpu.roll(into[k], 8, axis=1) for k in range(4)]
    square = jnp.concatenate(parts + [jnp.zeros((96, 128), F32)], axis=0)
    mix = square.T[0:16, :]
    high = rounded(mix)
    mix = (high + pltpu.roll(high, 32, axis=1) + pltpu.roll(mix - high, 64, axis=1)).astype(BF16)[:, 0:96]

    def combined(r, a):
        cols = [
            jnp.concatenate([X[k, pl.ds((a + b) * ROWS + r, NV, stride=BLK), :] for k in range(4)], axis=0)
            for b in range(2)
        ]
        wide = jnp.concatenate(cols, axis=1)
        high = rounded(wide)
        stacked = jnp.concatenate([high, wide - high, high], axis=0).astype(BF16)
        return jnp.dot(mix, stacked, preferred_element_type=F32)

    def finish(r, c):
        for a in (0, 2):
            out = combined(r, a)
            for b in range(2):
                o_sc[pl.ds(r * AZL + a + b, NV, stride=RC * AZL), :] = out[0:8, b * 128 : b * 128 + 128]
                o_rc[pl.ds(r * AZL + a + b, NV, stride=RC * AZL), :] = out[8:16, b * 128 : b * 128 + 128]
        return c

    lax.fori_loop(0, RC, finish, 0, unroll=4)

    def finish_shell(r, c):
        for a in (0, 2):
            out = combined(RC + r, a)
            for b in range(2):
                o_ss[pl.ds(r * AZL + a + b, NV, stride=RS * AZL), :] = out[0:8, b * 128 : b * 128 + 128]
                o_rs[pl.ds(r * AZL + a + b, NV, stride=RS * AZL), :] = out[8:16, b * 128 : b * 128 + 128]
        return c

    lax.fori_loop(0, RS, finish_shell, 0, unroll=2)

    stores = [
        pltpu.make_async_copy(src, dst, out_sem.at[i])
        for i, (src, dst) in enumerate([(o_sc, sol_c), (o_rc, res_c), (o_ss, sol_s), (o_rs, res_s)])
    ]
    for store in stores:
        store.start()
    for k in range(STEPS):
        sent(k)
    for store in stores:
        store.wait()


def per_device(cavity_block, shell_block, column_matrix, shell_matrix, shifted_diagonal, shell_diagonal, wet_area):
    nc, ns = NV * RC * AZL, NV * RS * AZL
    anywhere = pl.BlockSpec(memory_space=pl.ANY)
    outs = pl.pallas_call(
        kernel,
        out_shape=(
            jax.ShapeDtypeStruct((nc, 128), F32),
            jax.ShapeDtypeStruct((nc, 128), F32),
            jax.ShapeDtypeStruct((ns, 128), F32),
            jax.ShapeDtypeStruct((ns, 128), F32),
        ),
        in_specs=[anywhere] * 7,
        out_specs=(anywhere,) * 4,
        scratch_shapes=[
            pltpu.VMEM((4, NV * BLK, 128), F32),
            pltpu.VMEM((STEPS, NV, ROWS, 128), F32),
            pltpu.VMEM((STEPS, NV, ROWS, 128), F32),
            pltpu.VMEM((STEPS, NV, BLK, 128), F32),
            pltpu.VMEM((STEPS, NV, 8, 128), F32),
            pltpu.VMEM((STEPS, NV, 8, 128), F32),
            pltpu.VMEM((AZL, ROWS, 128), F32),
            pltpu.VMEM((64, 256), BF16),
            pltpu.VMEM((64, 128), F32),
            pltpu.VMEM((128, 128), F32),
            pltpu.VMEM((16, 8, 128), F32),
            pltpu.VMEM((16, 8, 128), F32),
            pltpu.VMEM((nc, 128), F32),
            pltpu.VMEM((ns, 128), F32),
            pltpu.VMEM((RC * AZL, 128), F32),
            pltpu.VMEM((RS * AZL, 128), F32),
            pltpu.VMEM((AZL, 128), F32),
            pltpu.VMEM((RC, RC), F32),
            pltpu.VMEM((RS, RS), F32),
            pltpu.VMEM((nc, 128), F32),
            pltpu.VMEM((nc, 128), F32),
            pltpu.VMEM((ns, 128), F32),
            pltpu.VMEM((ns, 128), F32),
            pltpu.SemaphoreType.DMA((7,)),
            pltpu.SemaphoreType.DMA((4,)),
            pltpu.SemaphoreType.DMA((STEPS, 4)),
            pltpu.SemaphoreType.DMA((STEPS, NV, 4)),
            pltpu.SemaphoreType.DMA((16,)),
            pltpu.SemaphoreType.DMA((16,)),
            pltpu.SemaphoreType.DMA((16,)),
            pltpu.SemaphoreType.DMA((16,)),
        ],
        compiler_params=pltpu.CompilerParams(
            collective_id=0, has_side_effects=True, vmem_limit_bytes=32 * 1024 * 1024
        ),
        name="block_cg",
    )(
        cavity_block.reshape(nc, 128),
        shell_block.reshape(ns, 128),
        column_matrix.reshape(RC, RC),
        shell_matrix,
        shifted_diagonal.reshape(RC * AZL, 128),
        shell_diagonal.reshape(RS * AZL, 128),
        wet_area,
    )
    return (
        outs[0].reshape(NV, RC, AZL, 128),
        outs[1].reshape(NV, RC, AZL, 128),
        outs[2].reshape(NV, RS, AZL, 128),
        outs[3].reshape(NV, RS, AZL, 128),
    )


def solution(mesh):
    return jax.shard_map(
        per_device,
        mesh=mesh,
        in_specs=(
            P(None, "grp", "az", "ax"),
            P(None, None, "az", "ax"),
            P("grp", None, None),
            P(),
            P("grp", "az", "ax"),
            P(None, "az", "ax"),
            P("az", "ax"),
        ),
        out_specs=(
            P(None, "grp", "az", "ax"),
            P(None, "grp", "az", "ax"),
            P(None, None, "az", "ax"),
            P(None, None, "az", "ax"),
        ),
        check_vma=False,
    )
```

```python
import jax
import jax.numpy as jnp
from jax import lax
from jax.experimental import pallas as pl
from jax.experimental.pallas import tpu as pltpu
from jax.sharding import PartitionSpec as P

NV = 8
RC = 48
RS = 6
ROWS = 56
AZL = 4
BLK = AZL * ROWS
STEPS = 3
THETA = 9.0
MESH = pl.DeviceIdType.MESH
F32 = jnp.float32
BF16 = jnp.bfloat16


def rounded(value):
    return value.astype(BF16).astype(F32)


def kernel(
    cav, shl, colm, shm, dia, sdia, wet,
    X, MIX,
    HL, HR, SB, IS, IR, DG, W, STG, ACC, RX1, RX2,
    raw_c, raw_s, raw_d, raw_sd, raw_w, raw_cm, raw_sm,
    in_sem, send_sem, recv_sem, s1, r1, s2, r2,
):
    grp = lax.axis_index("grp")
    az = lax.axis_index("az")
    ax = lax.axis_index("ax")
    naz = 64
    right = lax.rem(az + 1, naz)
    left = lax.rem(az + naz - 1, naz)
    px = az // 16
    pz = lax.rem(az // 4, 4)
    py = lax.rem(az, 4)

    loads = [
        pltpu.make_async_copy(src, dst, in_sem.at[i])
        for i, (src, dst) in enumerate(
            [(cav, raw_c), (shl, raw_s), (dia, raw_d), (sdia, raw_sd), (wet, raw_w), (colm, raw_cm), (shm, raw_sm)]
        )
    ]
    for load in loads:
        load.start()

    barrier = pltpu.get_barrier_semaphore()

    def hello(where):
        pl.semaphore_signal(barrier, inc=1, device_id=where, device_id_type=MESH)

    me1 = px * 4 + py
    me2 = grp * 8 + pz * 2 + ax

    def peer1(d):
        s = lax.rem(me1 + d, 16)
        return s, {"grp": grp, "az": (s // 4) * 16 + pz * 4 + lax.rem(s, 4), "ax": ax}

    def peer2(d):
        s = lax.rem(me2 + d, 16)
        return s, {"grp": s // 8, "az": px * 16 + lax.rem(s // 2, 4) * 4 + py, "ax": lax.rem(s, 2)}

    to_right = {"grp": grp, "az": right, "ax": ax}
    to_left = {"grp": grp, "az": left, "ax": ax}
    to_core = {"grp": grp, "az": az, "ax": 1 - ax}
    to_half = {"grp": 1 - grp, "az": az, "ax": ax}
    for where in (to_right, to_left, to_core, to_half):
        hello(where)

    def hello_peers(d, c):
        hello(peer1(d)[1])
        hello(peer2(d)[1])
        return c

    lax.fori_loop(1, 16, hello_peers, 0)

    outer = (grp == 1).astype(F32)
    is_outer = grp == 1
    lane = lax.broadcasted_iota(jnp.int32, (8, 128), 1)
    row = lax.broadcasted_iota(jnp.int32, (8, 128), 0)

    for load in loads:
        load.wait()

    def place(v, c):
        for a in range(AZL):
            at = v * BLK + a * ROWS
            X[0, pl.ds(pl.multiple_of(at, 8), RC), :] = raw_c[pl.ds(v * (RC * AZL) + a, RC, stride=AZL), :]
            tail = jnp.concatenate(
                [raw_s[pl.ds(v * (RS * AZL) + a, RS, stride=AZL), :], jnp.zeros((2, 128), F32)], axis=0
            )
            X[0, pl.ds(pl.multiple_of(at + RC, 8), 8), :] = tail
        return c

    lax.fori_loop(0, NV, place, 0)

    def rows_to_send(k, v):
        for a in range(AZL):
            at = v * BLK + a * ROWS
            first = X[k, pl.ds(pl.multiple_of(at, 8), 8), :][0:1]
            last = X[k, pl.ds(pl.multiple_of(at + 40, 8), 8), :][7:8]
            IS[k, v, a : a + 1, :] = jnp.where(is_outer, first, last)
            IS[k, v, 4 + a : 5 + a, :] = last

    def exchange(k, v):
        base = pl.multiple_of(v * BLK, 8)
        top = pl.multiple_of(v * BLK + 3 * ROWS, 8)
        return (
            pltpu.make_async_remote_copy(
                X.at[k, pl.ds(top, ROWS), :], HL.at[k, v], send_sem.at[k, 0], recv_sem.at[k, v, 0],
                device_id=to_right, device_id_type=MESH,
            ),
            pltpu.make_async_remote_copy(
                X.at[k, pl.ds(base, ROWS), :], HR.at[k, v], send_sem.at[k, 1], recv_sem.at[k, v, 1],
                device_id=to_left, device_id_type=MESH,
            ),
            pltpu.make_async_remote_copy(
                X.at[k, pl.ds(base, BLK), :], SB.at[k, v], send_sem.at[k, 2], recv_sem.at[k, v, 2],
                device_id=to_core, device_id_type=MESH,
            ),
            pltpu.make_async_remote_copy(
                IS.at[k, v], IR.at[k, v], send_sem.at[k, 3], recv_sem.at[k, v, 3],
                device_id=to_half, device_id_type=MESH,
            ),
        )

    def sent(k):
        for i, (buf, where) in enumerate(((HL, to_right), (HR, to_left), (SB, to_core), (IS, to_half))):
            pltpu.make_async_remote_copy(
                buf.at[k], buf.at[k], send_sem.at[k, i], recv_sem.at[k, 0, i], device_id=where, device_id_type=MESH
            ).wait_send()

    pl.semaphore_wait(barrier, 34)

    def first_send(v, c):
        rows_to_send(0, v)
        for copy in exchange(0, v):
            copy.start()
        return c

    lax.fori_loop(0, NV, first_send, 0)

    for a in range(AZL):
        DG[a, 0:RC, :] = raw_d[pl.ds(a, RC, stride=AZL), :] + (4.0 - THETA)
        DG[a, RC:ROWS, :] = jnp.concatenate(
            [raw_sd[pl.ds(a, RS, stride=AZL), :] + (4.0 - THETA), jnp.zeros((2, 128), F32)], axis=0
        )
    STG[...] = jnp.zeros((64, 128), F32)
    STG[56:62, 0:RS] = raw_sm[...]
    shell_rows = pltpu.roll(STG[56:64, :], RC, axis=1)
    STG[56:64, :] = jnp.zeros((8, 128), F32)
    STG[0:RC, 0:RC] = raw_cm[...]
    STG[RC:ROWS, :] = shell_rows
    row64 = lax.broadcasted_iota(jnp.int32, (64, 128), 0)
    lane64 = lax.broadcasted_iota(jnp.int32, (64, 128), 1)
    iface = jnp.where(is_outer, 0, RC - 1)
    matrix = STG[...]
    matrix = jnp.where((lane64 == 56) & (row64 == iface), -1.0, matrix)
    matrix = jnp.where((lane64 == 57) & (row64 == RC), -1.0, matrix)
    matrix = jnp.where((lane64 == 58) & (row64 == RC - 1), -outer, matrix)
    high = rounded(matrix)
    W[...] = jnp.concatenate([high + pltpu.roll(high, 64, axis=1), matrix - high], axis=1).astype(BF16)

    lane56 = lax.broadcasted_iota(jnp.int32, (ROWS, 128), 1)
    first_lane = lane56 == 0
    last_lane = lane56 == 127
    from_left = (ax == 1).astype(F32)
    from_right = (ax == 0).astype(F32)
    share = 1.0 - outer

    def apply(k):
        def body(v, moments):
            base = v * BLK
            for copy in exchange(k, v):
                copy.wait_recv()
            own = [X[k, pl.ds(pl.multiple_of(base + a * ROWS, 8), ROWS), :] for a in range(AZL)]
            got = IR[k, v]
            spread = []
            for a in range(AZL):
                wet_row = raw_w[a : a + 1, :]
                wall = jnp.where(is_outer, own[a][RC - 1 : RC], got[4 + a : 5 + a])
                skin = own[a][RC : RC + 1]
                extra = jnp.where(row == 0, got[a : a + 1], 0.0)
                extra = jnp.where(row == 1, wet_row * wall, extra)
                extra = jnp.where(row == 2, wet_row * skin, extra)
                spread.append(jnp.concatenate([own[a], extra], axis=0))
            wide = jnp.concatenate(spread, axis=1)
            high = rounded(wide)
            stacked = jnp.concatenate([high, wide - high, high], axis=0).astype(BF16)
            mixed = jnp.dot(W[:, 0:192], stacked, preferred_element_type=F32)
            for a in range(AZL):
                side = SB[k, v, a * ROWS : (a + 1) * ROWS, :]
                before = HL[k, v] if a == 0 else own[a - 1]
                after = HR[k, v] if a == AZL - 1 else own[a + 1]
                lower = pltpu.roll(jnp.where(last_lane, side * from_left, own[a]), 1, axis=1)
                upper = pltpu.roll(jnp.where(first_lane, side * from_right, own[a]), 127, axis=1)
                new = mixed[0:ROWS, a * 128 : (a + 1) * 128] + DG[a] * own[a]
                new = new - ((before + after) + (lower + upper))
                X[k + 1, pl.ds(pl.multiple_of(base + a * ROWS, 8), ROWS), :] = new
            if k + 1 < STEPS:
                rows_to_send(k + 1, v)
                for copy in exchange(k + 1, v):
                    copy.start()
            even = [jnp.zeros((8, 128), F32) for _ in range(NV)]
            odd = [jnp.zeros((8, 128), F32) for _ in range(NV)]
            for p in range(BLK // 8):
                here = pl.ds(pl.multiple_of(base + p * 8, 8), 8)
                old, new = X[k, here, :], X[k + 1, here, :]
                if p % 7 == 6:
                    old, new = old * share, new * share
                for w in range(NV):
                    other = X[k, w * BLK + p * 8 : w * BLK + p * 8 + 8, :]
                    even[w] += other * old
                    odd[w] += other * new
            for w in range(NV):
                ACC[w * 8 : w * 8 + 8, :] = even[w]
                ACC[64 + w * 8 : 72 + w * 8, :] = odd[w]
            for half in range(2):
                total = ACC[pl.ds(64 * half, 8, stride=8), :]
                for s in range(1, 8):
                    total += ACC[pl.ds(64 * half + s, 8, stride=8), :]
                total = jnp.sum(total, axis=1, keepdims=True)
                moments = jnp.where(lane == 8 * (2 * k + half) + v, total, moments)
            return moments

        return body

    moments = jnp.zeros((8, 128), F32)
    for k in range(STEPS):
        moments = lax.fori_loop(0, NV, apply(k), moments)

    def total_of(value, me, peer, buf, ssem, rsem):
        buf[me] = value

        def copy_of(d):
            s, where = peer(d)
            return s, pltpu.make_async_remote_copy(
                buf.at[me], buf.at[me], ssem.at[d], rsem.at[me], device_id=where, device_id_type=MESH
            )

        def start(d, c):
            copy_of(d)[1].start()
            return c

        def wait(d, c):
            s, where = peer(d)
            pltpu.make_async_remote_copy(
                buf.at[s], buf.at[s], ssem.at[d], rsem.at[s], device_id=where, device_id_type=MESH
            ).wait_recv()
            return c

        def drain(d, c):
            copy_of(d)[1].wait_send()
            return c

        lax.fori_loop(1, 16, start, 0)
        lax.fori_loop(1, 16, wait, 0)
        result = buf[0]
        for s in range(1, 16):
            result += buf[s]
        lax.fori_loop(1, 16, drain, 0)
        return result

    gram = total_of(moments, me1, peer1, RX1, s1, r1)
    gram = total_of(gram, me2, peer2, RX2, s2, r2)

    shifted = pltpu.roll(gram, 120, axis=1) + THETA * gram
    table = []
    for i in range(STEPS):
        left_part = shifted if i == 0 else pltpu.roll(shifted, 128 - 8 * i, axis=1)
        right_part = pltpu.roll(gram, 24 - 8 * i, axis=1)
        table.append(jnp.where(lane < 24, left_part, jnp.where(lane < 32, right_part, 0.0)))
    for p in range(8 * STEPS):
        at, r = p // 8, p % 8
        pivot_row = table[at][r : r + 1, :]
        scaled = pivot_row * (1.0 / pivot_row[:, p : p + 1])
        for i in range(STEPS):
            column = table[i][:, p : p + 1]
            reduced = table[i] - column * scaled
            table[i] = jnp.where(row == r, scaled, reduced) if i == at else reduced

    y = [jnp.where(lane < 8, pltpu.roll(t, 104, axis=1), 0.0) for t in table]
    eye = jnp.where(lane == row, 1.0, 0.0)
    into = [
        eye - THETA * y[0],
        -(y[0] + THETA * y[1]),
        -(y[1] + THETA * y[2]),
        -y[2],
    ]
    zero8 = jnp.zeros((8, 128), F32)
    parts = [(y[k] if k < STEPS else zero8) + pltpu.roll(into[k], 8, axis=1) for k in range(4)]
    square = jnp.concatenate(parts + [jnp.zeros((96, 128), F32)], axis=0)
    mix = square.T[0:16, :]
    high = rounded(mix)
    MIX[...] = high + pltpu.roll(high, 32, axis=1) + pltpu.roll(mix - high, 64, axis=1)
    for k in range(STEPS):
        sent(k)


PIECES = 4


def finish_kernel(X, MIX, sol_c, res_c, sol_s, res_s, o_sc, o_rc, o_ss, o_rs, sem):
    mix = MIX[...].astype(BF16)[:, 0:96]

    def combined(r, a):
        cols = [
            jnp.concatenate([X[k, pl.ds((a + b) * ROWS + r, NV, stride=BLK), :] for k in range(4)], axis=0)
            for b in range(2)
        ]
        wide = jnp.concatenate(cols, axis=1)
        high = rounded(wide)
        stacked = jnp.concatenate([high, wide - high, high], axis=0).astype(BF16)
        return jnp.dot(mix, stacked, preferred_element_type=F32)

    def rows_of(first, rows, o_sol, o_res):
        def body(r, c):
            for a in (0, 2):
                out = combined(first + r, a)
                for b in range(2):
                    here = pl.ds(r * AZL + a + b, NV, stride=rows * AZL)
                    o_sol[here, :] = out[0:8, b * 128 : b * 128 + 128]
                    o_res[here, :] = out[8:16, b * 128 : b * 128 + 128]
            return c

        return body

    def piece(i, o, dst, slot, rows):
        copies = []
        for v in range(NV):
            here = pl.ds(v * RC * AZL + i * rows, rows)
            copies.append(pltpu.make_async_copy(o.at[here, :], dst.at[here, :], sem.at[slot]))
        return copies

    each = RC // PIECES
    lax.fori_loop(0, RS, rows_of(RC, RS, o_ss, o_rs), 0, unroll=2)
    small = [
        pltpu.make_async_copy(o_ss, sol_s, sem.at[2]),
        pltpu.make_async_copy(o_rs, res_s, sem.at[3]),
    ]
    for copy in small:
        copy.start()
    for i in range(PIECES):
        lax.fori_loop(i * each, (i + 1) * each, rows_of(0, RC, o_sc, o_rc), 0, unroll=4)
        for copy in piece(i, o_sc, sol_c, 0, each * AZL) + piece(i, o_rc, res_c, 1, each * AZL):
            copy.start()
    for copy in small:
        copy.wait()
    pltpu.make_async_copy(o_sc, sol_c, sem.at[0]).wait()
    pltpu.make_async_copy(o_rc, res_c, sem.at[1]).wait()


def per_device(cavity_block, shell_block, column_matrix, shell_matrix, shifted_diagonal, shell_diagonal, wet_area):
    nc, ns = NV * RC * AZL, NV * RS * AZL
    anywhere = pl.BlockSpec(memory_space=pl.ANY)
    args = (
        cavity_block.reshape(nc, 128),
        shell_block.reshape(ns, 128),
        column_matrix.reshape(RC, RC),
        shell_matrix,
        shifted_diagonal.reshape(RC * AZL, 128),
        shell_diagonal.reshape(RS * AZL, 128),
        wet_area,
    )
    args = [pltpu.with_memory_space_constraint(x, pltpu.HBM) for x in args]
    inside = pl.BlockSpec(memory_space=pltpu.VMEM)
    basis, mix = pl.pallas_call(
        kernel,
        out_shape=(pltpu.VMEM((4, NV * BLK, 128), F32), pltpu.VMEM((16, 128), F32)),
        in_specs=[anywhere] * 7,
        out_specs=(inside, inside),
        scratch_shapes=[
            pltpu.VMEM((STEPS, NV, ROWS, 128), F32),
            pltpu.VMEM((STEPS, NV, ROWS, 128), F32),
            pltpu.VMEM((STEPS, NV, BLK, 128), F32),
            pltpu.VMEM((STEPS, NV, 8, 128), F32),
            pltpu.VMEM((STEPS, NV, 8, 128), F32),
            pltpu.VMEM((AZL, ROWS, 128), F32),
            pltpu.VMEM((64, 256), BF16),
            pltpu.VMEM((64, 128), F32),
            pltpu.VMEM((128, 128), F32),
            pltpu.VMEM((16, 8, 128), F32),
            pltpu.VMEM((16, 8, 128), F32),
            pltpu.VMEM((nc, 128), F32),
            pltpu.VMEM((ns, 128), F32),
            pltpu.VMEM((RC * AZL, 128), F32),
            pltpu.VMEM((RS * AZL, 128), F32),
            pltpu.VMEM((AZL, 128), F32),
            pltpu.VMEM((RC, RC), F32),
            pltpu.VMEM((RS, RS), F32),
            pltpu.SemaphoreType.DMA((7,)),
            pltpu.SemaphoreType.DMA((STEPS, 4)),
            pltpu.SemaphoreType.DMA((STEPS, NV, 4)),
            pltpu.SemaphoreType.DMA((16,)),
            pltpu.SemaphoreType.DMA((16,)),
            pltpu.SemaphoreType.DMA((16,)),
            pltpu.SemaphoreType.DMA((16,)),
        ],
        compiler_params=pltpu.CompilerParams(
            collective_id=0, has_side_effects=True, vmem_limit_bytes=24 * 1024 * 1024
        ),
        name="block_cg",
    )(*args)
    outs = pl.pallas_call(
        finish_kernel,
        out_shape=(
            jax.ShapeDtypeStruct((nc, 128), F32),
            jax.ShapeDtypeStruct((nc, 128), F32),
            jax.ShapeDtypeStruct((ns, 128), F32),
            jax.ShapeDtypeStruct((ns, 128), F32),
        ),
        in_specs=[inside, inside],
        out_specs=(anywhere,) * 4,
        scratch_shapes=[
            pltpu.VMEM((nc, 128), F32),
            pltpu.VMEM((nc, 128), F32),
            pltpu.VMEM((ns, 128), F32),
            pltpu.VMEM((ns, 128), F32),
            pltpu.SemaphoreType.DMA((4,)),
        ],
        compiler_params=pltpu.CompilerParams(vmem_limit_bytes=24 * 1024 * 1024),
        name="combine_basis",
    )(
        pltpu.with_memory_space_constraint(basis, pltpu.VMEM),
        pltpu.with_memory_space_constraint(mix, pltpu.VMEM),
    )
    return (
        outs[0].reshape(NV, RC, AZL, 128),
        outs[1].reshape(NV, RC, AZL, 128),
        outs[2].reshape(NV, RS, AZL, 128),
        outs[3].reshape(NV, RS, AZL, 128),
    )


def solution(mesh):
    return jax.shard_map(
        per_device,
        mesh=mesh,
        in_specs=(
            P(None, "grp", "az", "ax"),
            P(None, None, "az", "ax"),
            P("grp", None, None),
            P(),
            P("grp", "az", "ax"),
            P(None, "az", "ax"),
            P("az", "ax"),
        ),
        out_specs=(
            P(None, "grp", "az", "ax"),
            P(None, "grp", "az", "ax"),
            P(None, None, "az", "ax"),
            P(None, None, "az", "ax"),
        ),
        check_vma=False,
    )
```

```python
import jax
import jax.numpy as jnp
from jax import lax
from jax.experimental import pallas as pl
from jax.experimental.pallas import tpu as pltpu
from jax.sharding import PartitionSpec as P

NV = 8
RC = 48
RS = 6
ROWS = 56
AZL = 4
BLK = AZL * ROWS
STEPS = 3
THETA = 9.0
MESH = pl.DeviceIdType.MESH
F32 = jnp.float32
BF16 = jnp.bfloat16


def rounded(value):
    return value.astype(BF16).astype(F32)


def kernel(
    cav, shl, colm, shm, dia, sdia, wet,
    T, MIX,
    X, HL, HR, SB, IS, IR, WS, WR, DG, W, STG, ACC, RX,
    raw_c, raw_s, raw_d, raw_sd, raw_w, raw_cm, raw_sm,
    in_sem, send_sem, recv_sem, sum_send, sum_recv,
):
    grp = lax.axis_index("grp")
    az = lax.axis_index("az")
    ax = lax.axis_index("ax")
    naz = 64
    right = lax.rem(az + 1, naz)
    left = lax.rem(az + naz - 1, naz)
    px = az // 16
    pz = lax.rem(az // 4, 4)
    py = lax.rem(az, 4)

    loads = [
        pltpu.make_async_copy(src, dst, in_sem.at[i])
        for i, (src, dst) in enumerate(
            [(cav, raw_c), (shl, raw_s), (dia, raw_d), (sdia, raw_sd), (wet, raw_w), (colm, raw_cm), (shm, raw_sm)]
        )
    ]
    for load in loads:
        load.start()

    barrier = pltpu.get_barrier_semaphore()

    def hello(where):
        pl.semaphore_signal(barrier, inc=1, device_id=where, device_id_type=MESH)

    me1 = px * 4 + py
    me2 = grp * 8 + pz * 2 + ax

    def peer1(d):
        s = lax.rem(me1 + d, 16)
        return s, {"grp": grp, "az": (s // 4) * 16 + pz * 4 + lax.rem(s, 4), "ax": ax}

    def peer2(d):
        s = lax.rem(me2 + d, 16)
        return s, {"grp": s // 8, "az": px * 16 + lax.rem(s // 2, 4) * 4 + py, "ax": lax.rem(s, 2)}

    to_right = {"grp": grp, "az": right, "ax": ax}
    to_left = {"grp": grp, "az": left, "ax": ax}
    to_core = {"grp": grp, "az": az, "ax": 1 - ax}
    to_half = {"grp": 1 - grp, "az": az, "ax": ax}
    for where in (to_right, to_left, to_core, to_half):
        hello(where)

    def hello_peers(d, c):
        hello(peer1(d)[1])
        hello(peer2(d)[1])
        return c

    lax.fori_loop(1, 16, hello_peers, 0)

    outer = (grp == 1).astype(F32)
    is_outer = grp == 1
    lane = lax.broadcasted_iota(jnp.int32, (8, 128), 1)
    row = lax.broadcasted_iota(jnp.int32, (8, 128), 0)

    def rows_to_send(k, v):
        for a in range(AZL):
            at = v * BLK + a * ROWS
            first = X[k, pl.ds(pl.multiple_of(at, 8), 8), :][0:1]
            last = X[k, pl.ds(pl.multiple_of(at + 40, 8), 8), :][7:8]
            IS[k, v, a : a + 1, :] = jnp.where(is_outer, first, last)
            WS[k, v, a : a + 1, :] = last

    def exchange(k, v):
        base = pl.multiple_of(v * BLK, 8)
        top = pl.multiple_of(v * BLK + 3 * ROWS, 8)
        return (
            pltpu.make_async_remote_copy(
                X.at[k, pl.ds(top, ROWS), :], HL.at[k, v], send_sem.at[k, 0], recv_sem.at[k, v, 0],
                device_id=to_right, device_id_type=MESH,
            ),
            pltpu.make_async_remote_copy(
                X.at[k, pl.ds(base, ROWS), :], HR.at[k, v], send_sem.at[k, 1], recv_sem.at[k, v, 1],
                device_id=to_left, device_id_type=MESH,
            ),
            pltpu.make_async_remote_copy(
                X.at[k, pl.ds(base, BLK), :], SB.at[k, v], send_sem.at[k, 2], recv_sem.at[k, v, 2],
                device_id=to_core, device_id_type=MESH,
            ),
            pltpu.make_async_remote_copy(
                IS.at[k, v], IR.at[k, v], send_sem.at[k, 3], recv_sem.at[k, v, 3],
                device_id=to_half, device_id_type=MESH,
            ),
        )

    def wall_copy(k, v):
        return pltpu.make_async_remote_copy(
            WS.at[k, v], WR.at[k, v], send_sem.at[k, 4], recv_sem.at[k, v, 4], device_id=to_half, device_id_type=MESH
        )

    def send(k, v):
        rows_to_send(k, v)
        for copy in exchange(k, v):
            copy.start()

        @pl.when(is_outer)
        def _():
            wall_copy(k, v).start()

    def sent(k):
        def all_of(i, buf, where):
            pltpu.make_async_remote_copy(
                buf.at[k], buf.at[k], send_sem.at[k, i], recv_sem.at[k, 0, i], device_id=where, device_id_type=MESH
            ).wait_send()

        for i, (buf, where) in enumerate(((HL, to_right), (HR, to_left), (SB, to_core), (IS, to_half))):
            all_of(i, buf, where)

        @pl.when(is_outer)
        def _():
            all_of(4, WS, to_half)

    pl.semaphore_wait(barrier, 34)

    for load in loads[:2]:
        load.wait()

    def first_send(v, c):
        for a in range(AZL):
            at = v * BLK + a * ROWS
            X[0, pl.ds(pl.multiple_of(at, 8), RC), :] = raw_c[pl.ds(v * (RC * AZL) + a, RC, stride=AZL), :]
            tail = jnp.concatenate(
                [raw_s[pl.ds(v * (RS * AZL) + a, RS, stride=AZL), :], jnp.zeros((2, 128), F32)], axis=0
            )
            X[0, pl.ds(pl.multiple_of(at + RC, 8), 8), :] = tail
        send(0, v)
        return c

    lax.fori_loop(0, NV, first_send, 0)
    for load in loads[2:]:
        load.wait()

    for a in range(AZL):
        DG[a, 0:RC, :] = raw_d[pl.ds(a, RC, stride=AZL), :] + (4.0 - THETA)
        DG[a, RC:ROWS, :] = jnp.concatenate(
            [raw_sd[pl.ds(a, RS, stride=AZL), :] + (4.0 - THETA), jnp.zeros((2, 128), F32)], axis=0
        )
    STG[...] = jnp.zeros((64, 128), F32)
    STG[56:62, 0:RS] = raw_sm[...]
    shell_rows = pltpu.roll(STG[56:64, :], RC, axis=1)
    STG[56:64, :] = jnp.zeros((8, 128), F32)
    STG[0:RC, 0:RC] = raw_cm[...]
    STG[RC:ROWS, :] = shell_rows
    row64 = lax.broadcasted_iota(jnp.int32, (64, 128), 0)
    lane64 = lax.broadcasted_iota(jnp.int32, (64, 128), 1)
    iface = jnp.where(is_outer, 0, RC - 1)
    matrix = STG[...]
    matrix = jnp.where((lane64 == 56) & (row64 == iface), -1.0, matrix)
    matrix = jnp.where((lane64 == 57) & (row64 == RC), -1.0, matrix)
    matrix = jnp.where((lane64 == 58) & (row64 == RC - 1), -outer, matrix)
    high = rounded(matrix)
    W[...] = jnp.concatenate([high + pltpu.roll(high, 64, axis=1), matrix - high], axis=1).astype(BF16)

    lane56 = lax.broadcasted_iota(jnp.int32, (ROWS, 128), 1)
    first_lane = lane56 == 0
    last_lane = lane56 == 127
    from_left = (ax == 1).astype(F32)
    from_right = (ax == 0).astype(F32)
    share = 1.0 - outer

    def apply(k):
        def body(v, moments):
            base = v * BLK
            for copy in exchange(k, v):
                copy.wait_recv()

            @pl.when(grp == 0)
            def _():
                wall_copy(k, v).wait_recv()

            own = [X[k, pl.ds(pl.multiple_of(base + a * ROWS, 8), ROWS), :] for a in range(AZL)]
            got, far = IR[k, v], WR[k, v]
            spread = []
            for a in range(AZL):
                wet_row = raw_w[a : a + 1, :]
                wall = jnp.where(is_outer, own[a][RC - 1 : RC], far[a : a + 1])
                skin = own[a][RC : RC + 1]
                extra = jnp.where(row == 0, got[a : a + 1], 0.0)
                extra = jnp.where(row == 1, wet_row * wall, extra)
                extra = jnp.where(row == 2, wet_row * skin, extra)
                spread.append(jnp.concatenate([own[a], extra], axis=0))
            wide = jnp.concatenate(spread, axis=1)
            high = rounded(wide)
            stacked = jnp.concatenate([high, wide - high, high], axis=0).astype(BF16)
            mixed = jnp.dot(W[:, 0:192], stacked, preferred_element_type=F32)
            for a in range(AZL):
                side = SB[k, v, a * ROWS : (a + 1) * ROWS, :]
                before = HL[k, v] if a == 0 else own[a - 1]
                after = HR[k, v] if a == AZL - 1 else own[a + 1]
                lower = pltpu.roll(jnp.where(last_lane, side * from_left, own[a]), 1, axis=1)
                upper = pltpu.roll(jnp.where(first_lane, side * from_right, own[a]), 127, axis=1)
                new = mixed[0:ROWS, a * 128 : (a + 1) * 128] + DG[a] * own[a]
                new = new - ((before + after) + (lower + upper))
                X[k + 1, pl.ds(pl.multiple_of(base + a * ROWS, 8), ROWS), :] = new
            if k + 1 < STEPS:
                send(k + 1, v)
                which = [(k, k, 16 * k), (k, k + 1, 16 * k + 8)]
            else:
                which = [(k, k + 1, 16)]
            return products(which, v, moments)

        return body

    def products(which, v, moments):
        k = which[0][0]
        base = v * BLK
        sums = [[jnp.zeros((8, 128), F32) for _ in range(NV)] for _ in which]
        for p in range(BLK // 8):
            here = pl.ds(pl.multiple_of(base + p * 8, 8), 8)
            mine = [X[j, here, :] for _, j, _ in which]
            if p % 7 == 6:
                mine = [m * share for m in mine]
            for w in range(NV):
                other = X[k, w * BLK + p * 8 : w * BLK + p * 8 + 8, :]
                for q in range(len(which)):
                    sums[q][w] += other * mine[q]
        for q, (_, _, at) in enumerate(which):
            for w in range(NV):
                ACC[64 * q + w * 8 : 64 * q + w * 8 + 8, :] = sums[q][w]
            total = ACC[pl.ds(64 * q, 8, stride=8), :]
            for s in range(1, 8):
                total += ACC[pl.ds(64 * q + s, 8, stride=8), :]
            total = jnp.sum(total, axis=1, keepdims=True)
            moments = jnp.where(lane == at + v, total, moments)
        return moments

    def copy_of(i, d):
        me, (s, where) = (me1, peer1(d)) if i % 2 == 0 else (me2, peer2(d))
        out = pltpu.make_async_remote_copy(
            RX.at[i, me], RX.at[i, me], sum_send.at[i, d], sum_recv.at[i, me], device_id=where, device_id_type=MESH
        )
        back = pltpu.make_async_remote_copy(
            RX.at[i, s], RX.at[i, s], sum_send.at[i, d], sum_recv.at[i, s], device_id=where, device_id_type=MESH
        )
        return out, back

    def sum_start(i, value):
        RX[i, me1 if i % 2 == 0 else me2] = value

        def start(d, c):
            copy_of(i, d)[0].start()
            return c

        lax.fori_loop(1, 16, start, 0)

    def sum_finish(i):
        def wait(d, c):
            copy_of(i, d)[1].wait_recv()
            return c

        lax.fori_loop(1, 16, wait, 0)
        result = RX[i, 0]
        for s in range(1, 16):
            result += RX[i, s]
        return result

    def sum_drain(i):
        def drain(d, c):
            copy_of(i, d)[0].wait_send()
            return c

        lax.fori_loop(1, 16, drain, 0)

    def prepare(r, c):
        for half in range(2):
            cols = [
                jnp.concatenate(
                    [X[k, pl.ds((2 * half + b) * ROWS + r, NV, stride=BLK), :] for k in range(4)], axis=0
                )
                for b in range(2)
            ]
            wide = jnp.concatenate(cols, axis=1)
            high = rounded(wide)
            T[2 * r + half] = jnp.concatenate([high, wide - high, high], axis=0).astype(BF16)
        return c

    zero8 = jnp.zeros((8, 128), F32)
    early = lax.fori_loop(0, NV, apply(0), zero8)
    early = lax.fori_loop(0, NV, apply(1), early)
    early = lax.fori_loop(0, NV, lambda v, m: products([(2, 2, 32)], v, m), early)
    sum_start(0, early)
    late = lax.fori_loop(0, NV, apply(2), zero8)
    sum_start(2, late)
    early = sum_finish(0)
    sum_start(1, early)
    lax.fori_loop(0, 27, prepare, 0, unroll=3)
    late = sum_finish(2)
    sum_start(3, late)
    gram = sum_finish(1)
    shifted = pltpu.roll(gram, 120, axis=1) + THETA * gram
    table = []
    for i in range(STEPS):
        left_part = shifted if i == 0 else pltpu.roll(shifted, 128 - 8 * i, axis=1)
        right_part = pltpu.roll(gram, 24 - 8 * i, axis=1)
        table.append(jnp.where(lane < 24, left_part, jnp.where(lane < 32, right_part, 0.0)))
    for p in range(8 * STEPS):
        at, r = p // 8, p % 8
        if p == 16:
            lax.fori_loop(27, 54, prepare, 0, unroll=3)
            table[2] = table[2] + sum_finish(3)
        pivot_row = table[at][r : r + 1, :]
        scaled = pivot_row * (1.0 / pivot_row[:, p : p + 1])
        for i in range(STEPS):
            column = table[i][:, p : p + 1]
            reduced = table[i] - column * scaled
            table[i] = jnp.where(row == r, scaled, reduced) if i == at else reduced

    y = [jnp.where(lane < 8, pltpu.roll(t, 104, axis=1), 0.0) for t in table]
    eye = jnp.where(lane == row, 1.0, 0.0)
    into = [
        eye - THETA * y[0],
        -(y[0] + THETA * y[1]),
        -(y[1] + THETA * y[2]),
        -y[2],
    ]
    parts = [(y[k] if k < STEPS else zero8) + pltpu.roll(into[k], 8, axis=1) for k in range(4)]
    square = jnp.concatenate(parts + [jnp.zeros((96, 128), F32)], axis=0)
    mix = square.T[0:16, :]
    high = rounded(mix)
    MIX[...] = high + pltpu.roll(high, 32, axis=1) + pltpu.roll(mix - high, 64, axis=1)
    for k in range(STEPS):
        sent(k)
    for i in range(4):
        sum_drain(i)


PIECES = 4


def finish_kernel(T, MIX, sol_c, res_c, sol_s, res_s, o_sc, o_rc, o_ss, o_rs, sem):
    mix = MIX[...].astype(BF16)[:, 0:96]

    def rows_of(first, rows, o_sol, o_res):
        def body(r, c):
            for a in (0, 2):
                out = jnp.dot(mix, T[2 * (first + r) + a // 2], preferred_element_type=F32)
                for b in range(2):
                    here = pl.ds(r * AZL + a + b, NV, stride=rows * AZL)
                    o_sol[here, :] = out[0:8, b * 128 : b * 128 + 128]
                    o_res[here, :] = out[8:16, b * 128 : b * 128 + 128]
            return c

        return body

    def piece(i, o, dst, slot, rows):
        copies = []
        for v in range(NV):
            here = pl.ds(v * RC * AZL + i * rows, rows)
            copies.append(pltpu.make_async_copy(o.at[here, :], dst.at[here, :], sem.at[slot]))
        return copies

    each = RC // PIECES
    lax.fori_loop(0, RS, rows_of(RC, RS, o_ss, o_rs), 0, unroll=2)
    small = [
        pltpu.make_async_copy(o_ss, sol_s, sem.at[2]),
        pltpu.make_async_copy(o_rs, res_s, sem.at[3]),
    ]
    for copy in small:
        copy.start()
    for i in range(PIECES):
        lax.fori_loop(i * each, (i + 1) * each, rows_of(0, RC, o_sc, o_rc), 0, unroll=4)
        for copy in piece(i, o_sc, sol_c, 0, each * AZL) + piece(i, o_rc, res_c, 1, each * AZL):
            copy.start()
    for copy in small:
        copy.wait()
    pltpu.make_async_copy(o_sc, sol_c, sem.at[0]).wait()
    pltpu.make_async_copy(o_rc, res_c, sem.at[1]).wait()


def per_device(cavity_block, shell_block, column_matrix, shell_matrix, shifted_diagonal, shell_diagonal, wet_area):
    nc, ns = NV * RC * AZL, NV * RS * AZL
    anywhere = pl.BlockSpec(memory_space=pl.ANY)
    args = (
        cavity_block.reshape(nc, 128),
        shell_block.reshape(ns, 128),
        column_matrix.reshape(RC, RC),
        shell_matrix,
        shifted_diagonal.reshape(RC * AZL, 128),
        shell_diagonal.reshape(RS * AZL, 128),
        wet_area,
    )
    args = [pltpu.with_memory_space_constraint(x, pltpu.HBM) for x in args]
    inside = pl.BlockSpec(memory_space=pltpu.VMEM)
    basis, mix = pl.pallas_call(
        kernel,
        out_shape=(pltpu.VMEM((2 * (RC + RS), 96, 256), BF16), pltpu.VMEM((16, 128), F32)),
        in_specs=[anywhere] * 7,
        out_specs=(inside, inside),
        scratch_shapes=[
            pltpu.VMEM((4, NV * BLK, 128), F32),
            pltpu.VMEM((STEPS, NV, ROWS, 128), F32),
            pltpu.VMEM((STEPS, NV, ROWS, 128), F32),
            pltpu.VMEM((STEPS, NV, BLK, 128), F32),
            pltpu.VMEM((STEPS, NV, AZL, 128), F32),
            pltpu.VMEM((STEPS, NV, AZL, 128), F32),
            pltpu.VMEM((STEPS, NV, AZL, 128), F32),
            pltpu.VMEM((STEPS, NV, AZL, 128), F32),
            pltpu.VMEM((AZL, ROWS, 128), F32),
            pltpu.VMEM((64, 256), BF16),
            pltpu.VMEM((64, 128), F32),
            pltpu.VMEM((128, 128), F32),
            pltpu.VMEM((4, 16, 8, 128), F32),
            pltpu.VMEM((nc, 128), F32),
            pltpu.VMEM((ns, 128), F32),
            pltpu.VMEM((RC * AZL, 128), F32),
            pltpu.VMEM((RS * AZL, 128), F32),
            pltpu.VMEM((AZL, 128), F32),
            pltpu.VMEM((RC, RC), F32),
            pltpu.VMEM((RS, RS), F32),
            pltpu.SemaphoreType.DMA((7,)),
            pltpu.SemaphoreType.DMA((STEPS, 5)),
            pltpu.SemaphoreType.DMA((STEPS, NV, 5)),
            pltpu.SemaphoreType.DMA((4, 16)),
            pltpu.SemaphoreType.DMA((4, 16)),
        ],
        compiler_params=pltpu.CompilerParams(
            collective_id=0, has_side_effects=True, vmem_limit_bytes=22 * 1024 * 1024
        ),
        name="block_cg",
    )(*args)
    outs = pl.pallas_call(
        finish_kernel,
        out_shape=(
            jax.ShapeDtypeStruct((nc, 128), F32),
            jax.ShapeDtypeStruct((nc, 128), F32),
            jax.ShapeDtypeStruct((ns, 128), F32),
            jax.ShapeDtypeStruct((ns, 128), F32),
        ),
        in_specs=[inside, inside],
        out_specs=(anywhere,) * 4,
        scratch_shapes=[
            pltpu.VMEM((nc, 128), F32),
            pltpu.VMEM((nc, 128), F32),
            pltpu.VMEM((ns, 128), F32),
            pltpu.VMEM((ns, 128), F32),
            pltpu.SemaphoreType.DMA((4,)),
        ],
        compiler_params=pltpu.CompilerParams(vmem_limit_bytes=22 * 1024 * 1024),
        name="combine_basis",
    )(
        pltpu.with_memory_space_constraint(basis, pltpu.VMEM),
        pltpu.with_memory_space_constraint(mix, pltpu.VMEM),
    )
    return (
        outs[0].reshape(NV, RC, AZL, 128),
        outs[1].reshape(NV, RC, AZL, 128),
        outs[2].reshape(NV, RS, AZL, 128),
        outs[3].reshape(NV, RS, AZL, 128),
    )


def solution(mesh):
    return jax.shard_map(
        per_device,
        mesh=mesh,
        in_specs=(
            P(None, "grp", "az", "ax"),
            P(None, None, "az", "ax"),
            P("grp", None, None),
            P(),
            P("grp", "az", "ax"),
            P(None, "az", "ax"),
            P("az", "ax"),
        ),
        out_specs=(
            P(None, "grp", "az", "ax"),
            P(None, "grp", "az", "ax"),
            P(None, None, "az", "ax"),
            P(None, None, "az", "ax"),
        ),
        check_vma=False,
    )
```

```python
import jax
import jax.numpy as jnp
from jax import lax
from jax.experimental import pallas as pl
from jax.experimental.pallas import tpu as pltpu
from jax.sharding import PartitionSpec as P

NV = 8
RC = 48
RS = 6
ROWS = 56
LAYER = RC + RS
AZL = 4
BLK = AZL * ROWS
STEPS = 3
THETA = 9.0
MESH = pl.DeviceIdType.MESH
F32 = jnp.float32
BF16 = jnp.bfloat16


def rounded(value):
    return value.astype(BF16).astype(F32)


def kernel(
    cav, shl, colm, shm, dia, sdia, wet,
    T, MIX,
    X, HL, HR, SB, IS, IR, WS, WR, DG, W, STG, ACC, RX,
    raw_c, raw_s, raw_d, raw_sd, raw_w, raw_cm, raw_sm,
    in_sem, vec_sem, send_sem, recv_sem, sum_send, sum_recv,
):
    grp = lax.axis_index("grp")
    az = lax.axis_index("az")
    ax = lax.axis_index("ax")
    naz = 64
    right = lax.rem(az + 1, naz)
    left = lax.rem(az + naz - 1, naz)
    px = az // 16
    pz = lax.rem(az // 4, 4)
    py = lax.rem(az, 4)

    loads = [
        pltpu.make_async_copy(src, dst, in_sem.at[i])
        for i, (src, dst) in enumerate(
            [(shl, raw_s), (dia, raw_d), (sdia, raw_sd), (wet, raw_w), (colm, raw_cm), (shm, raw_sm)]
        )
    ]
    def load_vector(v):
        here = pl.ds(pl.multiple_of(v * (RC * AZL), 8), RC * AZL)
        return pltpu.make_async_copy(cav.at[here, :], raw_c.at[here, :], vec_sem.at[v])

    loads[0].start()
    for v in range(NV):
        load_vector(v).start()
    for load in loads[1:]:
        load.start()

    barrier = pltpu.get_barrier_semaphore()

    def hello(where):
        pl.semaphore_signal(barrier, inc=1, device_id=where, device_id_type=MESH)

    here1 = px * 4 + py
    here2 = grp * 4 + pz
    slots = (16, 8, 2)

    def place_in(stage):
        return (here1, here2, ax)[stage]

    def peer(stage, d):
        if stage == 0:
            x, y = lax.rem(px + d // 4, 4), lax.rem(py + d % 4, 4)
            return x * 4 + y, {"grp": grp, "az": x * 16 + pz * 4 + y, "ax": ax}
        if stage == 1:
            g, z = lax.rem(grp + d // 4, 2), lax.rem(pz + d % 4, 4)
            return g * 4 + z, {"grp": g, "az": px * 16 + z * 4 + py, "ax": ax}
        return 1 - ax, {"grp": grp, "az": az, "ax": 1 - ax}

    to_right = {"grp": grp, "az": right, "ax": ax}
    to_left = {"grp": grp, "az": left, "ax": ax}
    to_core = {"grp": grp, "az": az, "ax": 1 - ax}
    to_half = {"grp": 1 - grp, "az": az, "ax": ax}
    for where in (to_right, to_left, to_core, to_half):
        hello(where)

    for stage in range(2):
        for d in range(1, slots[stage]):
            hello(peer(stage, d)[1])

    outer = (grp == 1).astype(F32)
    is_outer = grp == 1
    lane = lax.broadcasted_iota(jnp.int32, (8, 128), 1)
    row = lax.broadcasted_iota(jnp.int32, (8, 128), 0)

    def rows_to_send(k, v):
        for a in range(AZL):
            at = v * BLK + a * ROWS
            first = X[k, pl.ds(pl.multiple_of(at, 8), 8), :][0:1]
            last = X[k, pl.ds(pl.multiple_of(at + 40, 8), 8), :][7:8]
            IS[k, v, a : a + 1, :] = jnp.where(is_outer, first, last)
            WS[k, v, a : a + 1, :] = last

    def exchange(k, v):
        base = pl.multiple_of(v * BLK, 8)
        top = pl.multiple_of(v * BLK + 3 * ROWS, 8)
        return (
            pltpu.make_async_remote_copy(
                X.at[k, pl.ds(top, LAYER), :], HL.at[k, v, pl.ds(0, LAYER), :], send_sem.at[k, 0], recv_sem.at[k, v, 0],
                device_id=to_right, device_id_type=MESH,
            ),
            pltpu.make_async_remote_copy(
                X.at[k, pl.ds(base, LAYER), :], HR.at[k, v, pl.ds(0, LAYER), :], send_sem.at[k, 1], recv_sem.at[k, v, 1],
                device_id=to_left, device_id_type=MESH,
            ),
            pltpu.make_async_remote_copy(
                X.at[k, pl.ds(base, BLK), :], SB.at[k, v], send_sem.at[k, 2], recv_sem.at[k, v, 2],
                device_id=to_core, device_id_type=MESH,
            ),
            pltpu.make_async_remote_copy(
                IS.at[k, v], IR.at[k, v], send_sem.at[k, 3], recv_sem.at[k, v, 3],
                device_id=to_half, device_id_type=MESH,
            ),
        )

    def wall_copy(k, v):
        return pltpu.make_async_remote_copy(
            WS.at[k, v], WR.at[k, v], send_sem.at[k, 4], recv_sem.at[k, v, 4], device_id=to_half, device_id_type=MESH
        )

    def send(k, v):
        rows_to_send(k, v)
        for copy in exchange(k, v):
            copy.start()

        @pl.when(is_outer)
        def _():
            wall_copy(k, v).start()

    def sent(k):
        def all_of(i, buf, where):
            pltpu.make_async_remote_copy(
                buf.at[k], buf.at[k], send_sem.at[k, i], recv_sem.at[k, 0, i], device_id=where, device_id_type=MESH
            ).wait_send()

        for i, (buf, where) in enumerate(((HL, to_right), (HR, to_left), (SB, to_core), (IS, to_half))):
            part = LAYER if i < 2 else buf.shape[2]
            all_of(i, buf.at[:, :, pl.ds(0, part), :], where)

        @pl.when(is_outer)
        def _():
            all_of(4, WS, to_half)

    def no_padding(v, c):
        for k in range(STEPS):
            HL[k, v, LAYER:ROWS, :] = jnp.zeros((ROWS - LAYER, 128), F32)
            HR[k, v, LAYER:ROWS, :] = jnp.zeros((ROWS - LAYER, 128), F32)
        return c

    lax.fori_loop(0, NV, no_padding, 0)
    pl.semaphore_wait(barrier, 26)

    loads[0].wait()

    def first_send(v, c):
        load_vector(v).wait()
        for a in range(AZL):
            at = v * BLK + a * ROWS
            X[0, pl.ds(pl.multiple_of(at, 8), RC), :] = raw_c[pl.ds(v * (RC * AZL) + a, RC, stride=AZL), :]
            tail = jnp.concatenate(
                [raw_s[pl.ds(v * (RS * AZL) + a, RS, stride=AZL), :], jnp.zeros((2, 128), F32)], axis=0
            )
            X[0, pl.ds(pl.multiple_of(at + RC, 8), 8), :] = tail
        send(0, v)
        return c

    lax.fori_loop(0, NV, first_send, 0)
    for load in loads[1:]:
        load.wait()

    for a in range(AZL):
        DG[a, 0:RC, :] = raw_d[pl.ds(a, RC, stride=AZL), :] + (4.0 - THETA)
        DG[a, RC:ROWS, :] = jnp.concatenate(
            [raw_sd[pl.ds(a, RS, stride=AZL), :] + (4.0 - THETA), jnp.zeros((2, 128), F32)], axis=0
        )
    STG[...] = jnp.zeros((64, 128), F32)
    STG[56:62, 0:RS] = raw_sm[...]
    shell_rows = pltpu.roll(STG[56:64, :], RC, axis=1)
    STG[56:64, :] = jnp.zeros((8, 128), F32)
    STG[0:RC, 0:RC] = raw_cm[...]
    STG[RC:ROWS, :] = shell_rows
    row64 = lax.broadcasted_iota(jnp.int32, (64, 128), 0)
    lane64 = lax.broadcasted_iota(jnp.int32, (64, 128), 1)
    matrix = STG[...]
    matrix = jnp.where((lane64 == 58) & (row64 == RC - 1), -outer, matrix)
    high = rounded(matrix)
    W[...] = jnp.concatenate([high + pltpu.roll(high, 64, axis=1), matrix - high], axis=1).astype(BF16)

    lane56 = lax.broadcasted_iota(jnp.int32, (ROWS, 128), 1)
    first_lane = lane56 == 0
    last_lane = lane56 == 127
    from_left = (ax == 1).astype(F32)
    from_right = (ax == 0).astype(F32)
    share = 1.0 - outer

    def apply(k):
        def body(v, moments):
            base = v * BLK
            from_left_slab, from_right_slab, from_core, from_half = exchange(k, v)
            from_core.wait_recv()
            own = [X[k, pl.ds(pl.multiple_of(base + a * ROWS, 8), ROWS), :] for a in range(AZL)]
            wet_rows = [raw_w[a : a + 1, :] for a in range(AZL)]
            spread = []
            for a in range(AZL):
                extra = jnp.where(row == 2, wet_rows[a] * own[a][RC : RC + 1], 0.0)
                spread.append(jnp.concatenate([own[a], extra], axis=0))
            wide = jnp.concatenate(spread, axis=1)
            high = rounded(wide)
            stacked = jnp.concatenate([high, wide - high, high], axis=0).astype(BF16)
            mixed = jnp.dot(W[:, 0:192], stacked, preferred_element_type=F32)
            part = []
            for a in range(AZL):
                side = SB[k, v, a * ROWS : (a + 1) * ROWS, :]
                lower = pltpu.roll(jnp.where(last_lane, side * from_left, own[a]), 1, axis=1)
                upper = pltpu.roll(jnp.where(first_lane, side * from_right, own[a]), 127, axis=1)
                value = mixed[0:ROWS, a * 128 : (a + 1) * 128] + DG[a] * own[a] - (lower + upper)
                if a > 0:
                    value = value - own[a - 1]
                if a < AZL - 1:
                    value = value - own[a + 1]
                part.append(value)

            from_left_slab.wait_recv()
            from_right_slab.wait_recv()
            from_half.wait_recv()

            @pl.when(grp == 0)
            def _():
                wall_copy(k, v).wait_recv()

            got, far = IR[k, v], WR[k, v]
            for a in range(AZL):
                value = part[a]
                if a == 0:
                    value = value - HL[k, v]
                if a == AZL - 1:
                    value = value - HR[k, v]
                wall = jnp.where(is_outer, own[a][RC - 1 : RC], far[a : a + 1])
                at = base + a * ROWS
                top = value[0:8] - jnp.where(row == 0, outer * got[a : a + 1], 0.0)
                edge = value[40:48] - jnp.where(row == 7, share * got[a : a + 1], 0.0)
                skin = value[48:56] - jnp.where(row == 0, wet_rows[a] * wall, 0.0)
                X[k + 1, pl.ds(pl.multiple_of(at, 8), 8), :] = top
                X[k + 1, pl.ds(pl.multiple_of(at + 8, 8), 32), :] = value[8:40]
                X[k + 1, pl.ds(pl.multiple_of(at + 40, 8), 8), :] = edge
                X[k + 1, pl.ds(pl.multiple_of(at + 48, 8), 8), :] = skin
            if k + 1 < STEPS:
                send(k + 1, v)
                which = [(k, k, 16 * k), (k, k + 1, 16 * k + 8)]
            else:
                which = [(k, k + 1, 16)]
            return products(which, v, moments)

        return body

    def products(which, v, moments):
        k = which[0][0]
        base = v * BLK
        sums = [[jnp.zeros((8, 128), F32) for _ in range(NV)] for _ in which]
        for p in range(BLK // 8):
            here = pl.ds(pl.multiple_of(base + p * 8, 8), 8)
            mine = [X[j, here, :] for _, j, _ in which]
            if p % 7 == 6:
                mine = [m * share for m in mine]
            for w in range(NV):
                other = X[k, w * BLK + p * 8 : w * BLK + p * 8 + 8, :]
                for q in range(len(which)):
                    sums[q][w] += other * mine[q]
        for q, (_, _, at) in enumerate(which):
            for w in range(NV):
                ACC[64 * q + w * 8 : 64 * q + w * 8 + 8, :] = sums[q][w]
            total = ACC[pl.ds(64 * q, 8, stride=8), :]
            for s in range(1, 8):
                total += ACC[pl.ds(64 * q + s, 8, stride=8), :]
            total = jnp.sum(total, axis=1, keepdims=True)
            moments = jnp.where(lane == at + v, total, moments)
        return moments

    def sum_copy(i, stage, d):
        at = place_in(stage)
        return pltpu.make_async_remote_copy(
            RX.at[i, stage, at], RX.at[i, stage, at], sum_send.at[i, stage], sum_recv.at[i, stage],
            device_id=peer(stage, d)[1], device_id_type=MESH,
        )

    def sum_all(i, stage):
        n = slots[stage] - 1
        block = RX.at[i, stage, pl.ds(0, n)]
        return pltpu.make_async_remote_copy(
            block, block, sum_send.at[i, stage], sum_recv.at[i, stage],
            device_id=peer(stage, 1)[1], device_id_type=MESH,
        )

    def sum_start(i, stage, value):
        RX[i, stage, place_in(stage)] = value
        for d in range(1, slots[stage]):
            sum_copy(i, stage, d).start()

    def sum_finish(i, stage):
        sum_all(i, stage).wait_recv()
        terms = [RX[i, stage, s] for s in range(slots[stage])]
        while len(terms) > 1:
            terms = [terms[q] + terms[q + 1] for q in range(0, len(terms), 2)]
        return terms[0]

    def prepare(r, c):
        for half in range(2):
            cols = [
                jnp.concatenate(
                    [X[k, pl.ds((2 * half + b) * ROWS + r, NV, stride=BLK), :] for k in range(4)], axis=0
                )
                for b in range(2)
            ]
            wide = jnp.concatenate(cols, axis=1)
            high = rounded(wide)
            T[2 * r + half] = jnp.concatenate([high, wide - high, high], axis=0).astype(BF16)
        return c

    zero8 = jnp.zeros((8, 128), F32)
    early = lax.fori_loop(0, NV, apply(0), zero8)
    early = lax.fori_loop(0, NV, apply(1), early)
    early = lax.fori_loop(0, NV, lambda v, m: products([(2, 2, 32)], v, m), early)
    sum_start(0, 2, early)
    sum_start(0, 0, sum_finish(0, 2))
    late = lax.fori_loop(0, NV, apply(2), zero8)
    sum_start(1, 2, late)
    sum_start(1, 0, sum_finish(1, 2))
    sum_start(0, 1, sum_finish(0, 0))
    lax.fori_loop(0, 27, prepare, 0, unroll=3)
    sum_start(1, 1, sum_finish(1, 0))
    gram = sum_finish(0, 1)

    shifted = pltpu.roll(gram, 120, axis=1) + THETA * gram
    table = []
    for i in range(STEPS):
        left_part = shifted if i == 0 else pltpu.roll(shifted, 128 - 8 * i, axis=1)
        right_part = pltpu.roll(gram, 24 - 8 * i, axis=1)
        table.append(jnp.where(lane < 24, left_part, jnp.where(lane < 32, right_part, 0.0)))
    for p in range(8 * STEPS):
        at, r = p // 8, p % 8
        if p == 16:
            lax.fori_loop(27, 54, prepare, 0, unroll=3)
            for k in range(STEPS):
                sent(k)
            for i, stage in ((0, 2), (0, 0), (0, 1), (1, 2), (1, 0)):
                sum_all(i, stage).wait_send()
            table[2] = table[2] + sum_finish(1, 1)
        pivot_row = table[at][r : r + 1, :]
        scaled = pivot_row * (1.0 / pivot_row[:, p : p + 1])
        for i in range(STEPS):
            column = table[i][:, p : p + 1]
            reduced = table[i] - column * scaled
            table[i] = jnp.where(row == r, scaled, reduced) if i == at else reduced

    y = [jnp.where(lane < 8, pltpu.roll(t, 104, axis=1), 0.0) for t in table]
    eye = jnp.where(lane == row, 1.0, 0.0)
    into = [
        eye - THETA * y[0],
        -(y[0] + THETA * y[1]),
        -(y[1] + THETA * y[2]),
        -y[2],
    ]
    parts = [(y[k] if k < STEPS else zero8) + pltpu.roll(into[k], 8, axis=1) for k in range(4)]
    square = jnp.concatenate(parts + [jnp.zeros((96, 128), F32)], axis=0)
    mix = square.T[0:16, :]
    high = rounded(mix)
    MIX[...] = high + pltpu.roll(high, 32, axis=1) + pltpu.roll(mix - high, 64, axis=1)
    sum_all(1, 1).wait_send()


PIECES = 4


def finish_kernel(T, MIX, sol_c, res_c, sol_s, res_s, o_sc, o_rc, o_ss, o_rs, sem):
    mix = MIX[...].astype(BF16)[:, 0:96]

    def rows_of(first, rows, o_sol, o_res):
        def body(r, c):
            for a in (0, 2):
                out = jnp.dot(mix, T[2 * (first + r) + a // 2], preferred_element_type=F32)
                for b in range(2):
                    here = pl.ds(r * AZL + a + b, NV, stride=rows * AZL)
                    o_sol[here, :] = out[0:8, b * 128 : b * 128 + 128]
                    o_res[here, :] = out[8:16, b * 128 : b * 128 + 128]
            return c

        return body

    def piece(i, o, dst, slot, rows):
        copies = []
        for v in range(NV):
            here = pl.ds(v * RC * AZL + i * rows, rows)
            copies.append(pltpu.make_async_copy(o.at[here, :], dst.at[here, :], sem.at[slot]))
        return copies

    each = RC // PIECES
    lax.fori_loop(0, RS, rows_of(RC, RS, o_ss, o_rs), 0, unroll=True)
    small = [
        pltpu.make_async_copy(o_ss, sol_s, sem.at[2]),
        pltpu.make_async_copy(o_rs, res_s, sem.at[3]),
    ]
    for copy in small:
        copy.start()
    for i in range(PIECES):
        lax.fori_loop(i * each, (i + 1) * each, rows_of(0, RC, o_sc, o_rc), 0, unroll=True)
        for copy in piece(i, o_sc, sol_c, 0, each * AZL) + piece(i, o_rc, res_c, 1, each * AZL):
            copy.start()
    for copy in small:
        copy.wait()
    pltpu.make_async_copy(o_sc, sol_c, sem.at[0]).wait()
    pltpu.make_async_copy(o_rc, res_c, sem.at[1]).wait()


def per_device(cavity_block, shell_block, column_matrix, shell_matrix, shifted_diagonal, shell_diagonal, wet_area):
    nc, ns = NV * RC * AZL, NV * RS * AZL
    anywhere = pl.BlockSpec(memory_space=pl.ANY)
    args = (
        cavity_block.reshape(nc, 128),
        shell_block.reshape(ns, 128),
        column_matrix.reshape(RC, RC),
        shell_matrix,
        shifted_diagonal.reshape(RC * AZL, 128),
        shell_diagonal.reshape(RS * AZL, 128),
        wet_area,
    )
    args = [pltpu.with_memory_space_constraint(x, pltpu.HBM) for x in args]
    inside = pl.BlockSpec(memory_space=pltpu.VMEM)
    basis, mix = pl.pallas_call(
        kernel,
        out_shape=(pltpu.VMEM((2 * (RC + RS), 96, 256), BF16), pltpu.VMEM((16, 128), F32)),
        in_specs=[anywhere] * 7,
        out_specs=(inside, inside),
        scratch_shapes=[
            pltpu.VMEM((4, NV * BLK, 128), F32),
            pltpu.VMEM((STEPS, NV, ROWS, 128), F32),
            pltpu.VMEM((STEPS, NV, ROWS, 128), F32),
            pltpu.VMEM((STEPS, NV, BLK, 128), F32),
            pltpu.VMEM((STEPS, NV, AZL, 128), F32),
            pltpu.VMEM((STEPS, NV, AZL, 128), F32),
            pltpu.VMEM((STEPS, NV, AZL, 128), F32),
            pltpu.VMEM((STEPS, NV, AZL, 128), F32),
            pltpu.VMEM((AZL, ROWS, 128), F32),
            pltpu.VMEM((64, 256), BF16),
            pltpu.VMEM((64, 128), F32),
            pltpu.VMEM((128, 128), F32),
            pltpu.VMEM((2, 3, 16, 8, 128), F32),
            pltpu.VMEM((nc, 128), F32),
            pltpu.VMEM((ns, 128), F32),
            pltpu.VMEM((RC * AZL, 128), F32),
            pltpu.VMEM((RS * AZL, 128), F32),
            pltpu.VMEM((AZL, 128), F32),
            pltpu.VMEM((RC, RC), F32),
            pltpu.VMEM((RS, RS), F32),
            pltpu.SemaphoreType.DMA((6,)),
            pltpu.SemaphoreType.DMA((NV,)),
            pltpu.SemaphoreType.DMA((STEPS, 5)),
            pltpu.SemaphoreType.DMA((STEPS, NV, 5)),
            pltpu.SemaphoreType.DMA((2, 3)),
            pltpu.SemaphoreType.DMA((2, 3)),
        ],
        compiler_params=pltpu.CompilerParams(
            collective_id=0, has_side_effects=True, vmem_limit_bytes=22 * 1024 * 1024
        ),
        name="block_cg",
    )(*args)
    outs = pl.pallas_call(
        finish_kernel,
        out_shape=(
            jax.ShapeDtypeStruct((nc, 128), F32),
            jax.ShapeDtypeStruct((nc, 128), F32),
            jax.ShapeDtypeStruct((ns, 128), F32),
            jax.ShapeDtypeStruct((ns, 128), F32),
        ),
        in_specs=[inside, inside],
        out_specs=(anywhere,) * 4,
        scratch_shapes=[
            pltpu.VMEM((nc, 128), F32),
            pltpu.VMEM((nc, 128), F32),
            pltpu.VMEM((ns, 128), F32),
            pltpu.VMEM((ns, 128), F32),
            pltpu.SemaphoreType.DMA((4,)),
        ],
        compiler_params=pltpu.CompilerParams(vmem_limit_bytes=22 * 1024 * 1024),
        name="combine_basis",
    )(
        pltpu.with_memory_space_constraint(basis, pltpu.VMEM),
        pltpu.with_memory_space_constraint(mix, pltpu.VMEM),
    )
    return (
        outs[0].reshape(NV, RC, AZL, 128),
        outs[1].reshape(NV, RC, AZL, 128),
        outs[2].reshape(NV, RS, AZL, 128),
        outs[3].reshape(NV, RS, AZL, 128),
    )


def solution(mesh):
    return jax.shard_map(
        per_device,
        mesh=mesh,
        in_specs=(
            P(None, "grp", "az", "ax"),
            P(None, None, "az", "ax"),
            P("grp", None, None),
            P(),
            P("grp", "az", "ax"),
            P(None, "az", "ax"),
            P("az", "ax"),
        ),
        out_specs=(
            P(None, "grp", "az", "ax"),
            P(None, "grp", "az", "ax"),
            P(None, None, "az", "ax"),
            P(None, None, "az", "ax"),
        ),
        check_vma=False,
    )
```

```python
import jax
import jax.numpy as jnp
from jax import lax
from jax.experimental import pallas as pl
from jax.experimental.pallas import tpu as pltpu
from jax.sharding import PartitionSpec as P

NV = 8
RC = 48
RS = 6
ROWS = 56
LAYER = RC + RS
AZL = 4
BLK = AZL * ROWS
STEPS = 3
THETA = 9.0
MESH = pl.DeviceIdType.MESH
F32 = jnp.float32
BF16 = jnp.bfloat16


def rounded(value):
    return value.astype(BF16).astype(F32)


def kernel(
    cav, shl, colm, shm, dia, sdia, wet,
    T, MIX,
    X, HL, HR, SB, IS, IR, WS, WR, DG, W, STG, ACC, RX,
    raw_c, raw_s, raw_d, raw_sd, raw_w, raw_cm, raw_sm,
    in_sem, vec_sem, send_sem, recv_sem, sum_send, sum_recv, word,
):
    grp = lax.axis_index("grp")
    az = lax.axis_index("az")
    ax = lax.axis_index("ax")
    naz = 64
    right = lax.rem(az + 1, naz)
    left = lax.rem(az + naz - 1, naz)
    px = az // 16
    pz = lax.rem(az // 4, 4)
    py = lax.rem(az, 4)

    loads = [
        pltpu.make_async_copy(src, dst, in_sem.at[i])
        for i, (src, dst) in enumerate(
            [(shl, raw_s), (dia, raw_d), (sdia, raw_sd), (wet, raw_w), (colm, raw_cm), (shm, raw_sm)]
        )
    ]
    def load_vector(v):
        here = pl.ds(pl.multiple_of(v * (RC * AZL), 8), RC * AZL)
        return pltpu.make_async_copy(cav.at[here, :], raw_c.at[here, :], vec_sem.at[v])

    loads[0].start()
    for v in range(NV):
        load_vector(v).start()
    for load in loads[1:]:
        load.start()

    barrier = pltpu.get_barrier_semaphore()

    def hello(where):
        pl.semaphore_signal(barrier, inc=1, device_id=where, device_id_type=MESH)

    here1 = px * 4 + py
    here2 = grp * 4 + pz
    slots = (16, 8, 2)

    def place_in(stage):
        return (here1, here2, ax)[stage]

    def peer(stage, d):
        if stage == 0:
            x, y = lax.rem(px + d // 4, 4), lax.rem(py + d % 4, 4)
            return x * 4 + y, {"grp": grp, "az": x * 16 + pz * 4 + y, "ax": ax}
        if stage == 1:
            g, z = lax.rem(grp + d // 4, 2), lax.rem(pz + d % 4, 4)
            return g * 4 + z, {"grp": g, "az": px * 16 + z * 4 + py, "ax": ax}
        return 1 - ax, {"grp": grp, "az": az, "ax": 1 - ax}

    def far(step, side):
        apart = 2 ** (step + 1)
        return {"grp": grp, "az": lax.rem(az + (apart if side == 0 else naz - apart), naz), "ax": ax}

    def pass_word(step):
        for side in range(2):
            pl.semaphore_signal(word.at[step, side], inc=1, device_id=far(step, side), device_id_type=MESH)

    def hear_word(step):
        for side in range(2):
            pl.semaphore_wait(word.at[step, side], 1)

    to_right = {"grp": grp, "az": right, "ax": ax}
    to_left = {"grp": grp, "az": left, "ax": ax}
    to_core = {"grp": grp, "az": az, "ax": 1 - ax}
    to_half = {"grp": 1 - grp, "az": az, "ax": ax}
    for where in (to_right, to_left, to_core, to_half):
        hello(where)

    outer = (grp == 1).astype(F32)
    is_outer = grp == 1
    lane = lax.broadcasted_iota(jnp.int32, (8, 128), 1)
    row = lax.broadcasted_iota(jnp.int32, (8, 128), 0)

    def rows_to_send(k, v):
        for a in range(AZL):
            at = v * BLK + a * ROWS
            first = X[k, pl.ds(pl.multiple_of(at, 8), 8), :][0:1]
            last = X[k, pl.ds(pl.multiple_of(at + 40, 8), 8), :][7:8]
            IS[k, v, a : a + 1, :] = jnp.where(is_outer, first, last)
            WS[k, v, a : a + 1, :] = last

    def exchange(k, v):
        base = pl.multiple_of(v * BLK, 8)
        top = pl.multiple_of(v * BLK + 3 * ROWS, 8)
        return (
            pltpu.make_async_remote_copy(
                X.at[k, pl.ds(top, LAYER), :], HL.at[k, v, pl.ds(0, LAYER), :], send_sem.at[k, 0], recv_sem.at[k, v, 0],
                device_id=to_right, device_id_type=MESH,
            ),
            pltpu.make_async_remote_copy(
                X.at[k, pl.ds(base, LAYER), :], HR.at[k, v, pl.ds(0, LAYER), :], send_sem.at[k, 1], recv_sem.at[k, v, 1],
                device_id=to_left, device_id_type=MESH,
            ),
            pltpu.make_async_remote_copy(
                X.at[k, pl.ds(base, BLK), :], SB.at[k, v], send_sem.at[k, 2], recv_sem.at[k, v, 2],
                device_id=to_core, device_id_type=MESH,
            ),
            pltpu.make_async_remote_copy(
                IS.at[k, v], IR.at[k, v], send_sem.at[k, 3], recv_sem.at[k, v, 3],
                device_id=to_half, device_id_type=MESH,
            ),
        )

    def wall_copy(k, v):
        return pltpu.make_async_remote_copy(
            WS.at[k, v], WR.at[k, v], send_sem.at[k, 4], recv_sem.at[k, v, 4], device_id=to_half, device_id_type=MESH
        )

    def send(k, v):
        rows_to_send(k, v)
        for copy in exchange(k, v):
            copy.start()

        @pl.when(is_outer)
        def _():
            wall_copy(k, v).start()

    def sent(k):
        def all_of(i, buf, where):
            pltpu.make_async_remote_copy(
                buf.at[k], buf.at[k], send_sem.at[k, i], recv_sem.at[k, 0, i], device_id=where, device_id_type=MESH
            ).wait_send()

        for i, (buf, where) in enumerate(((HL, to_right), (HR, to_left), (SB, to_core), (IS, to_half))):
            part = LAYER if i < 2 else buf.shape[2]
            all_of(i, buf.at[:, :, pl.ds(0, part), :], where)

        @pl.when(is_outer)
        def _():
            all_of(4, WS, to_half)

    def no_padding(v, c):
        for k in range(STEPS):
            HL[k, v, LAYER:ROWS, :] = jnp.zeros((ROWS - LAYER, 128), F32)
            HR[k, v, LAYER:ROWS, :] = jnp.zeros((ROWS - LAYER, 128), F32)
        return c

    lax.fori_loop(0, NV, no_padding, 0)
    pl.semaphore_wait(barrier, 4)

    loads[0].wait()

    def first_send(v, c):
        load_vector(v).wait()
        for a in range(AZL):
            at = v * BLK + a * ROWS
            X[0, pl.ds(pl.multiple_of(at, 8), RC), :] = raw_c[pl.ds(v * (RC * AZL) + a, RC, stride=AZL), :]
            tail = jnp.concatenate(
                [raw_s[pl.ds(v * (RS * AZL) + a, RS, stride=AZL), :], jnp.zeros((2, 128), F32)], axis=0
            )
            X[0, pl.ds(pl.multiple_of(at + RC, 8), 8), :] = tail
        send(0, v)
        return c

    lax.fori_loop(0, NV, first_send, 0)
    for load in loads[1:]:
        load.wait()

    for a in range(AZL):
        DG[a, 0:RC, :] = raw_d[pl.ds(a, RC, stride=AZL), :] + (4.0 - THETA)
        DG[a, RC:ROWS, :] = jnp.concatenate(
            [raw_sd[pl.ds(a, RS, stride=AZL), :] + (4.0 - THETA), jnp.zeros((2, 128), F32)], axis=0
        )
    STG[...] = jnp.zeros((64, 128), F32)
    STG[56:62, 0:RS] = raw_sm[...]
    shell_rows = pltpu.roll(STG[56:64, :], RC, axis=1)
    STG[56:64, :] = jnp.zeros((8, 128), F32)
    STG[0:RC, 0:RC] = raw_cm[...]
    STG[RC:ROWS, :] = shell_rows
    row64 = lax.broadcasted_iota(jnp.int32, (64, 128), 0)
    lane64 = lax.broadcasted_iota(jnp.int32, (64, 128), 1)
    matrix = STG[...]
    matrix = jnp.where((lane64 == 58) & (row64 == RC - 1), -outer, matrix)
    high = rounded(matrix)
    W[...] = jnp.concatenate([high + pltpu.roll(high, 64, axis=1), matrix - high], axis=1).astype(BF16)

    lane56 = lax.broadcasted_iota(jnp.int32, (ROWS, 128), 1)
    first_lane = lane56 == 0
    last_lane = lane56 == 127
    from_left = (ax == 1).astype(F32)
    from_right = (ax == 0).astype(F32)
    share = 1.0 - outer

    def apply(k):
        def body(v, moments):
            base = v * BLK
            from_left_slab, from_right_slab, from_core, from_half = exchange(k, v)
            from_core.wait_recv()
            own = [X[k, pl.ds(pl.multiple_of(base + a * ROWS, 8), ROWS), :] for a in range(AZL)]
            wet_rows = [raw_w[a : a + 1, :] for a in range(AZL)]
            spread = []
            for a in range(AZL):
                extra = jnp.where(row == 2, wet_rows[a] * own[a][RC : RC + 1], 0.0)
                spread.append(jnp.concatenate([own[a], extra], axis=0))
            wide = jnp.concatenate(spread, axis=1)
            high = rounded(wide)
            stacked = jnp.concatenate([high, wide - high, high], axis=0).astype(BF16)
            mixed = jnp.dot(W[:, 0:192], stacked, preferred_element_type=F32)
            part = []
            for a in range(AZL):
                side = SB[k, v, a * ROWS : (a + 1) * ROWS, :]
                lower = pltpu.roll(jnp.where(last_lane, side * from_left, own[a]), 1, axis=1)
                upper = pltpu.roll(jnp.where(first_lane, side * from_right, own[a]), 127, axis=1)
                value = mixed[0:ROWS, a * 128 : (a + 1) * 128] + DG[a] * own[a] - (lower + upper)
                if a > 0:
                    value = value - own[a - 1]
                if a < AZL - 1:
                    value = value - own[a + 1]
                part.append(value)

            from_left_slab.wait_recv()
            from_right_slab.wait_recv()
            from_half.wait_recv()

            @pl.when(grp == 0)
            def _():
                wall_copy(k, v).wait_recv()

            got, far = IR[k, v], WR[k, v]
            for a in range(AZL):
                value = part[a]
                if a == 0:
                    value = value - HL[k, v]
                if a == AZL - 1:
                    value = value - HR[k, v]
                wall = jnp.where(is_outer, own[a][RC - 1 : RC], far[a : a + 1])
                at = base + a * ROWS
                top = value[0:8] - jnp.where(row == 0, outer * got[a : a + 1], 0.0)
                edge = value[40:48] - jnp.where(row == 7, share * got[a : a + 1], 0.0)
                skin = value[48:56] - jnp.where(row == 0, wet_rows[a] * wall, 0.0)
                X[k + 1, pl.ds(pl.multiple_of(at, 8), 8), :] = top
                X[k + 1, pl.ds(pl.multiple_of(at + 8, 8), 32), :] = value[8:40]
                X[k + 1, pl.ds(pl.multiple_of(at + 40, 8), 8), :] = edge
                X[k + 1, pl.ds(pl.multiple_of(at + 48, 8), 8), :] = skin
            if k + 1 < STEPS:
                send(k + 1, v)
            for hear, tell, when in (((None, 0, 0),), ((0, 1, 0), (1, 2, NV - 1)), ((2, 3, 4),))[k]:

                @pl.when(v == when)
                def _(hear=hear, tell=tell):
                    if hear is not None:
                        hear_word(hear)
                    pass_word(tell)

            return products([(k, k, 16 * k), (k, k + 1, 16 * k + 8)], v, moments)

        return body

    def products(which, v, moments):
        k = which[0][0]
        base = v * BLK
        sums = [[jnp.zeros((8, 128), F32) for _ in range(NV)] for _ in which]
        for p in range(BLK // 8):
            here = pl.ds(pl.multiple_of(base + p * 8, 8), 8)
            mine = [X[j, here, :] for _, j, _ in which]
            if p % 7 == 6:
                mine = [m * share for m in mine]
            for w in range(NV):
                other = X[k, w * BLK + p * 8 : w * BLK + p * 8 + 8, :]
                for q in range(len(which)):
                    sums[q][w] += other * mine[q]
        for q, (_, _, at) in enumerate(which):
            for w in range(NV):
                ACC[64 * q + w * 8 : 64 * q + w * 8 + 8, :] = sums[q][w]
            total = ACC[pl.ds(64 * q, 8, stride=8), :]
            for s in range(1, 8):
                total += ACC[pl.ds(64 * q + s, 8, stride=8), :]
            total = jnp.sum(total, axis=1, keepdims=True)
            moments = jnp.where(lane == at + v, total, moments)
        return moments

    def sum_copy(stage, d):
        at = place_in(stage)
        return pltpu.make_async_remote_copy(
            RX.at[stage, at], RX.at[stage, at], sum_send.at[stage], sum_recv.at[stage],
            device_id=peer(stage, d)[1], device_id_type=MESH,
        )

    def sum_all(stage):
        n = slots[stage] - 1
        block = RX.at[stage, pl.ds(0, n)]
        return pltpu.make_async_remote_copy(
            block, block, sum_send.at[stage], sum_recv.at[stage],
            device_id=peer(stage, 1)[1], device_id_type=MESH,
        )

    def sum_start(stage, value):
        RX[stage, place_in(stage)] = value
        for d in range(1, slots[stage]):
            sum_copy(stage, d).start()

    def sum_finish(stage):
        sum_all(stage).wait_recv()
        terms = [RX[stage, s] for s in range(slots[stage])]
        while len(terms) > 1:
            terms = [terms[q] + terms[q + 1] for q in range(0, len(terms), 2)]
        return terms[0]

    def prepare(r, c):
        for half in range(2):
            cols = [
                jnp.concatenate(
                    [X[k, pl.ds((2 * half + b) * ROWS + r, NV, stride=BLK), :] for k in range(4)], axis=0
                )
                for b in range(2)
            ]
            wide = jnp.concatenate(cols, axis=1)
            high = rounded(wide)
            T[2 * r + half] = jnp.concatenate([high, wide - high, high], axis=0).astype(BF16)
        return c

    zero8 = jnp.zeros((8, 128), F32)
    moments = zero8
    for k in range(STEPS):
        moments = lax.fori_loop(0, NV, apply(k), moments)
    sum_start(2, moments)
    hear_word(3)
    pl.semaphore_signal(word.at[4, 0], inc=1, device_id=to_half, device_id_type=MESH)
    sum_start(0, sum_finish(2))
    lax.fori_loop(0, 27, prepare, 0, unroll=3)
    for k in range(STEPS):
        sent(k)
    pl.semaphore_wait(word.at[4, 0], 1)
    sum_start(1, sum_finish(0))
    lax.fori_loop(27, 54, prepare, 0, unroll=3)
    for stage in (2, 0):
        sum_all(stage).wait_send()
    gram = sum_finish(1)

    shifted = pltpu.roll(gram, 120, axis=1) + THETA * gram
    table = []
    for i in range(STEPS):
        left_part = shifted if i == 0 else pltpu.roll(shifted, 128 - 8 * i, axis=1)
        right_part = pltpu.roll(gram, 24 - 8 * i, axis=1)
        table.append(jnp.where(lane < 24, left_part, jnp.where(lane < 32, right_part, 0.0)))
    full = (8, 128)

    def over(part):
        return jnp.broadcast_to(part, full)

    for p in range(0, 8 * STEPS, 2):
        at, r = p // 8, p % 8
        first = [over(t[:, p : p + 1]) for t in table]
        second = [over(t[:, p + 1 : p + 2]) for t in table]
        inverse = 1.0 / over(first[at][r : r + 1, :])
        row_a = over(table[at][r : r + 1, :]) * inverse
        ratio = over(second[at][r : r + 1, :]) * inverse
        below = over(first[at][r + 1 : r + 2, :])
        row_b = over(table[at][r + 1 : r + 2, :]) - below * row_a
        row_b = row_b * (1.0 / (over(second[at][r + 1 : r + 2, :]) - below * ratio))
        row_a = row_a - ratio * row_b
        for i in range(STEPS):
            reduced = table[i] - first[i] * row_a - second[i] * row_b
            if i == at:
                reduced = jnp.where(row == r, row_a, jnp.where(row == r + 1, row_b, reduced))
            table[i] = reduced

    y = [jnp.where(lane < 8, pltpu.roll(t, 104, axis=1), 0.0) for t in table]
    eye = jnp.where(lane == row, 1.0, 0.0)
    into = [
        eye - THETA * y[0],
        -(y[0] + THETA * y[1]),
        -(y[1] + THETA * y[2]),
        -y[2],
    ]
    parts = [(y[k] if k < STEPS else zero8) + pltpu.roll(into[k], 8, axis=1) for k in range(4)]
    square = jnp.concatenate(parts + [jnp.zeros((96, 128), F32)], axis=0)
    mix = square.T[0:16, :]
    high = rounded(mix)
    MIX[...] = high + pltpu.roll(high, 32, axis=1) + pltpu.roll(mix - high, 64, axis=1)
    sum_all(1).wait_send()


PIECES = 4


def finish_kernel(T, MIX, sol_c, res_c, sol_s, res_s, o_sc, o_rc, o_ss, o_rs, sem):
    mix = MIX[...].astype(BF16)[:, 0:96]

    def rows_of(first, rows, o_sol, o_res):
        def body(r, c):
            for a in (0, 2):
                out = jnp.dot(mix, T[2 * (first + r) + a // 2], preferred_element_type=F32)
                for b in range(2):
                    here = pl.ds(r * AZL + a + b, NV, stride=rows * AZL)
                    o_sol[here, :] = out[0:8, b * 128 : b * 128 + 128]
                    o_res[here, :] = out[8:16, b * 128 : b * 128 + 128]
            return c

        return body

    def piece(i, o, dst, slot, rows):
        copies = []
        for v in range(NV):
            here = pl.ds(v * RC * AZL + i * rows, rows)
            copies.append(pltpu.make_async_copy(o.at[here, :], dst.at[here, :], sem.at[slot]))
        return copies

    each = RC // PIECES
    lax.fori_loop(0, RS, rows_of(RC, RS, o_ss, o_rs), 0, unroll=True)
    small = [
        pltpu.make_async_copy(o_ss, sol_s, sem.at[2]),
        pltpu.make_async_copy(o_rs, res_s, sem.at[3]),
    ]
    for copy in small:
        copy.start()
    for i in range(PIECES):
        lax.fori_loop(i * each, (i + 1) * each, rows_of(0, RC, o_sc, o_rc), 0, unroll=True)
        for copy in piece(i, o_sc, sol_c, 0, each * AZL) + piece(i, o_rc, res_c, 1, each * AZL):
            copy.start()
    for copy in small:
        copy.wait()
    pltpu.make_async_copy(o_sc, sol_c, sem.at[0]).wait()
    pltpu.make_async_copy(o_rc, res_c, sem.at[1]).wait()


def per_device(cavity_block, shell_block, column_matrix, shell_matrix, shifted_diagonal, shell_diagonal, wet_area):
    nc, ns = NV * RC * AZL, NV * RS * AZL
    anywhere = pl.BlockSpec(memory_space=pl.ANY)
    args = (
        cavity_block.reshape(nc, 128),
        shell_block.reshape(ns, 128),
        column_matrix.reshape(RC, RC),
        shell_matrix,
        shifted_diagonal.reshape(RC * AZL, 128),
        shell_diagonal.reshape(RS * AZL, 128),
        wet_area,
    )
    args = [pltpu.with_memory_space_constraint(x, pltpu.HBM) for x in args]
    inside = pl.BlockSpec(memory_space=pltpu.VMEM)
    basis, mix = pl.pallas_call(
        kernel,
        out_shape=(pltpu.VMEM((2 * (RC + RS), 96, 256), BF16), pltpu.VMEM((16, 128), F32)),
        in_specs=[anywhere] * 7,
        out_specs=(inside, inside),
        scratch_shapes=[
            pltpu.VMEM((4, NV * BLK, 128), F32),
            pltpu.VMEM((STEPS, NV, ROWS, 128), F32),
            pltpu.VMEM((STEPS, NV, ROWS, 128), F32),
            pltpu.VMEM((STEPS, NV, BLK, 128), F32),
            pltpu.VMEM((STEPS, NV, AZL, 128), F32),
            pltpu.VMEM((STEPS, NV, AZL, 128), F32),
            pltpu.VMEM((STEPS, NV, AZL, 128), F32),
            pltpu.VMEM((STEPS, NV, AZL, 128), F32),
            pltpu.VMEM((AZL, ROWS, 128), F32),
            pltpu.VMEM((64, 256), BF16),
            pltpu.VMEM((64, 128), F32),
            pltpu.VMEM((128, 128), F32),
            pltpu.VMEM((3, 16, 8, 128), F32),
            pltpu.VMEM((nc, 128), F32),
            pltpu.VMEM((ns, 128), F32),
            pltpu.VMEM((RC * AZL, 128), F32),
            pltpu.VMEM((RS * AZL, 128), F32),
            pltpu.VMEM((AZL, 128), F32),
            pltpu.VMEM((RC, RC), F32),
            pltpu.VMEM((RS, RS), F32),
            pltpu.SemaphoreType.DMA((6,)),
            pltpu.SemaphoreType.DMA((NV,)),
            pltpu.SemaphoreType.DMA((STEPS, 5)),
            pltpu.SemaphoreType.DMA((STEPS, NV, 5)),
            pltpu.SemaphoreType.DMA((3,)),
            pltpu.SemaphoreType.DMA((3,)),
            pltpu.SemaphoreType.REGULAR((5, 2)),
        ],
        compiler_params=pltpu.CompilerParams(
            collective_id=0, has_side_effects=True, vmem_limit_bytes=22 * 1024 * 1024
        ),
        name="block_cg",
    )(*args)
    outs = pl.pallas_call(
        finish_kernel,
        out_shape=(
            jax.ShapeDtypeStruct((nc, 128), F32),
            jax.ShapeDtypeStruct((nc, 128), F32),
            jax.ShapeDtypeStruct((ns, 128), F32),
            jax.ShapeDtypeStruct((ns, 128), F32),
        ),
        in_specs=[inside, inside],
        out_specs=(anywhere,) * 4,
        scratch_shapes=[
            pltpu.VMEM((nc, 128), F32),
            pltpu.VMEM((nc, 128), F32),
            pltpu.VMEM((ns, 128), F32),
            pltpu.VMEM((ns, 128), F32),
            pltpu.SemaphoreType.DMA((4,)),
        ],
        compiler_params=pltpu.CompilerParams(vmem_limit_bytes=22 * 1024 * 1024),
        name="combine_basis",
    )(
        pltpu.with_memory_space_constraint(basis, pltpu.VMEM),
        pltpu.with_memory_space_constraint(mix, pltpu.VMEM),
    )
    return (
        outs[0].reshape(NV, RC, AZL, 128),
        outs[1].reshape(NV, RC, AZL, 128),
        outs[2].reshape(NV, RS, AZL, 128),
        outs[3].reshape(NV, RS, AZL, 128),
    )


def solution(mesh):
    return jax.shard_map(
        per_device,
        mesh=mesh,
        in_specs=(
            P(None, "grp", "az", "ax"),
            P(None, None, "az", "ax"),
            P("grp", None, None),
            P(),
            P("grp", "az", "ax"),
            P(None, "az", "ax"),
            P("az", "ax"),
        ),
        out_specs=(
            P(None, "grp", "az", "ax"),
            P(None, "grp", "az", "ax"),
            P(None, None, "az", "ax"),
            P(None, None, "az", "ax"),
        ),
        check_vma=False,
    )
```

```python
import jax
import jax.numpy as jnp
from jax import lax
from jax.experimental import pallas as pl
from jax.experimental.pallas import tpu as pltpu
from jax.sharding import PartitionSpec as P

NV = 8
RC = 48
RS = 6
ROWS = 56
LAYER = RC + RS
AZL = 4
BLK = AZL * ROWS
STEPS = 3
THETA = 9.0
MESH = pl.DeviceIdType.MESH
F32 = jnp.float32
BF16 = jnp.bfloat16


def rounded(value):
    return value.astype(BF16).astype(F32)


def kernel(
    cav, shl, colm, shm, dia, sdia, wet,
    T, MIX,
    X, HL, HR, SB, IS, IR, WS, WR, DG, W, STG, ACC, RX,
    raw_c, raw_s, raw_d, raw_sd, raw_w, raw_cm, raw_sm,
    in_sem, vec_sem, send_sem, recv_sem, sum_send, sum_recv, word,
):
    grp = lax.axis_index("grp")
    az = lax.axis_index("az")
    ax = lax.axis_index("ax")
    naz = 64
    right = lax.rem(az + 1, naz)
    left = lax.rem(az + naz - 1, naz)
    px = az // 16
    pz = lax.rem(az // 4, 4)
    py = lax.rem(az, 4)

    barrier = pltpu.get_barrier_semaphore()

    def hello(where):
        pl.semaphore_signal(barrier, inc=1, device_id=where, device_id_type=MESH)

    here1 = px * 4 + py
    here2 = grp * 4 + pz
    slots = (16, 8, 2)

    def place_in(stage):
        return (here1, here2, ax)[stage]

    def peer(stage, d):
        if stage == 0:
            x, y = lax.rem(px + d // 4, 4), lax.rem(py + d % 4, 4)
            return x * 4 + y, {"grp": grp, "az": x * 16 + pz * 4 + y, "ax": ax}
        if stage == 1:
            g, z = lax.rem(grp + d // 4, 2), lax.rem(pz + d % 4, 4)
            return g * 4 + z, {"grp": g, "az": px * 16 + z * 4 + py, "ax": ax}
        return 1 - ax, {"grp": grp, "az": az, "ax": 1 - ax}

    def far(step, side):
        apart = 2 ** (step + 1)
        return {"grp": grp, "az": lax.rem(az + (apart if side == 0 else naz - apart), naz), "ax": ax}

    def pass_word(step):
        for side in range(2):
            pl.semaphore_signal(word.at[step, side], inc=1, device_id=far(step, side), device_id_type=MESH)

    def hear_word(step):
        for side in range(2):
            pl.semaphore_wait(word.at[step, side], 1)

    to_right = {"grp": grp, "az": right, "ax": ax}
    to_left = {"grp": grp, "az": left, "ax": ax}
    to_core = {"grp": grp, "az": az, "ax": 1 - ax}
    to_half = {"grp": 1 - grp, "az": az, "ax": ax}
    for where in (to_right, to_left, to_core, to_half):
        hello(where)

    loads = [
        pltpu.make_async_copy(src, dst, in_sem.at[i])
        for i, (src, dst) in enumerate(
            [(shl, raw_s), (dia, raw_d), (sdia, raw_sd), (wet, raw_w), (colm, raw_cm), (shm, raw_sm)]
        )
    ]
    def load_vector(v):
        here = pl.ds(pl.multiple_of(v * (RC * AZL), 8), RC * AZL)
        return pltpu.make_async_copy(cav.at[here, :], raw_c.at[here, :], vec_sem.at[v])

    loads[0].start()
    for v in range(NV):
        load_vector(v).start()
    for load in loads[1:]:
        load.start()

    outer = (grp == 1).astype(F32)
    is_outer = grp == 1
    lane = lax.broadcasted_iota(jnp.int32, (8, 128), 1)
    row = lax.broadcasted_iota(jnp.int32, (8, 128), 0)

    def rows_to_send(k, v):
        for a in range(AZL):
            at = v * BLK + a * ROWS
            first = X[k, pl.ds(pl.multiple_of(at, 8), 8), :][0:1]
            last = X[k, pl.ds(pl.multiple_of(at + 40, 8), 8), :][7:8]
            IS[k, v, a : a + 1, :] = jnp.where(is_outer, first, last)
            WS[k, v, a : a + 1, :] = last

    def exchange(k, v):
        base = pl.multiple_of(v * BLK, 8)
        top = pl.multiple_of(v * BLK + 3 * ROWS, 8)
        return (
            pltpu.make_async_remote_copy(
                X.at[k, pl.ds(top, LAYER), :], HL.at[k, v, pl.ds(0, LAYER), :], send_sem.at[k, 0], recv_sem.at[k, v, 0],
                device_id=to_right, device_id_type=MESH,
            ),
            pltpu.make_async_remote_copy(
                X.at[k, pl.ds(base, LAYER), :], HR.at[k, v, pl.ds(0, LAYER), :], send_sem.at[k, 1], recv_sem.at[k, v, 1],
                device_id=to_left, device_id_type=MESH,
            ),
            pltpu.make_async_remote_copy(
                X.at[k, pl.ds(base, BLK), :], SB.at[k, v], send_sem.at[k, 2], recv_sem.at[k, v, 2],
                device_id=to_core, device_id_type=MESH,
            ),
            pltpu.make_async_remote_copy(
                IS.at[k, v], IR.at[k, v], send_sem.at[k, 3], recv_sem.at[k, v, 3],
                device_id=to_half, device_id_type=MESH,
            ),
        )

    def wall_copy(k, v):
        return pltpu.make_async_remote_copy(
            WS.at[k, v], WR.at[k, v], send_sem.at[k, 4], recv_sem.at[k, v, 4], device_id=to_half, device_id_type=MESH
        )

    def send_layers(k, v):
        for copy in exchange(k, v)[:2]:
            copy.start()

    def send_rest(k, v):
        for copy in exchange(k, v)[2:]:
            copy.start()

        @pl.when(is_outer)
        def _():
            wall_copy(k, v).start()

    def sent(k):
        def all_of(i, buf, where):
            pltpu.make_async_remote_copy(
                buf.at[k], buf.at[k], send_sem.at[k, i], recv_sem.at[k, 0, i], device_id=where, device_id_type=MESH
            ).wait_send()

        for i, (buf, where) in enumerate(((HL, to_right), (HR, to_left), (SB, to_core), (IS, to_half))):
            part = LAYER if i < 2 else buf.shape[2]
            all_of(i, buf.at[:, :, pl.ds(0, part), :], where)

        @pl.when(is_outer)
        def _():
            all_of(4, WS, to_half)

    loads[0].wait()

    def settle(v, c):
        load_vector(v).wait()
        for a in range(AZL):
            at = v * BLK + a * ROWS
            X[0, pl.ds(pl.multiple_of(at, 8), RC), :] = raw_c[pl.ds(v * (RC * AZL) + a, RC, stride=AZL), :]
            tail = jnp.concatenate(
                [raw_s[pl.ds(v * (RS * AZL) + a, RS, stride=AZL), :], jnp.zeros((2, 128), F32)], axis=0
            )
            X[0, pl.ds(pl.multiple_of(at + RC, 8), 8), :] = tail
        rows_to_send(0, v)
        for k in range(STEPS):
            HL[k, v, LAYER:ROWS, :] = jnp.zeros((ROWS - LAYER, 128), F32)
            HR[k, v, LAYER:ROWS, :] = jnp.zeros((ROWS - LAYER, 128), F32)
        return c

    lax.fori_loop(0, NV, settle, 0)

    def first_send(v, c):
        send_layers(0, v)
        send_rest(0, v)
        return c

    pl.semaphore_wait(barrier, 4)
    lax.fori_loop(0, NV, first_send, 0)
    for load in loads[1:]:
        load.wait()

    for a in range(AZL):
        DG[a, 0:RC, :] = raw_d[pl.ds(a, RC, stride=AZL), :] + (4.0 - THETA)
        DG[a, RC:ROWS, :] = jnp.concatenate(
            [raw_sd[pl.ds(a, RS, stride=AZL), :] + (4.0 - THETA), jnp.zeros((2, 128), F32)], axis=0
        )
    STG[...] = jnp.zeros((64, 128), F32)
    STG[56:62, 0:RS] = raw_sm[...]
    shell_rows = pltpu.roll(STG[56:64, :], RC, axis=1)
    STG[56:64, :] = jnp.zeros((8, 128), F32)
    STG[0:RC, 0:RC] = raw_cm[...]
    STG[RC:ROWS, :] = shell_rows
    row64 = lax.broadcasted_iota(jnp.int32, (64, 128), 0)
    lane64 = lax.broadcasted_iota(jnp.int32, (64, 128), 1)
    matrix = STG[...]
    matrix = jnp.where((lane64 == 58) & (row64 == RC - 1), -outer, matrix)
    high = rounded(matrix)
    W[...] = jnp.concatenate([high + pltpu.roll(high, 64, axis=1), matrix - high], axis=1).astype(BF16)

    lane56 = lax.broadcasted_iota(jnp.int32, (ROWS, 128), 1)
    first_lane = lane56 == 0
    last_lane = lane56 == 127
    from_left = (ax == 1).astype(F32)
    from_right = (ax == 0).astype(F32)
    share = 1.0 - outer

    def apply(k):
        def body(v, moments):
            base = v * BLK
            from_left_slab, from_right_slab, from_core, from_half = exchange(k, v)
            from_core.wait_recv()
            own = [X[k, pl.ds(pl.multiple_of(base + a * ROWS, 8), ROWS), :] for a in range(AZL)]
            wet_rows = [raw_w[a : a + 1, :] for a in range(AZL)]
            spread = []
            for a in range(AZL):
                extra = jnp.where(row == 2, wet_rows[a] * own[a][RC : RC + 1], 0.0)
                spread.append(jnp.concatenate([own[a], extra], axis=0))
            wide = jnp.concatenate(spread, axis=1)
            high = rounded(wide)
            stacked = jnp.concatenate([high, wide - high, high], axis=0).astype(BF16)
            mixed = jnp.dot(W[:, 0:192], stacked, preferred_element_type=F32)
            part = []
            for a in range(AZL):
                side = SB[k, v, a * ROWS : (a + 1) * ROWS, :]
                lower = pltpu.roll(jnp.where(last_lane, side * from_left, own[a]), 1, axis=1)
                upper = pltpu.roll(jnp.where(first_lane, side * from_right, own[a]), 127, axis=1)
                value = mixed[0:ROWS, a * 128 : (a + 1) * 128] + DG[a] * own[a] - (lower + upper)
                if a > 0:
                    value = value - own[a - 1]
                if a < AZL - 1:
                    value = value - own[a + 1]
                part.append(value)

            from_left_slab.wait_recv()
            from_right_slab.wait_recv()
            from_half.wait_recv()

            @pl.when(grp == 0)
            def _():
                wall_copy(k, v).wait_recv()

            got, far = IR[k, v], WR[k, v]
            for a in (0, AZL - 1, *range(1, AZL - 1)):
                value = part[a]
                if a == 0:
                    value = value - HL[k, v]
                if a == AZL - 1:
                    value = value - HR[k, v]
                wall = jnp.where(is_outer, own[a][RC - 1 : RC], far[a : a + 1])
                at = base + a * ROWS
                top = value[0:8] - jnp.where(row == 0, outer * got[a : a + 1], 0.0)
                edge = value[40:48] - jnp.where(row == 7, share * got[a : a + 1], 0.0)
                skin = value[48:56] - jnp.where(row == 0, wet_rows[a] * wall, 0.0)
                X[k + 1, pl.ds(pl.multiple_of(at, 8), 8), :] = top
                X[k + 1, pl.ds(pl.multiple_of(at + 8, 8), 32), :] = value[8:40]
                X[k + 1, pl.ds(pl.multiple_of(at + 40, 8), 8), :] = edge
                X[k + 1, pl.ds(pl.multiple_of(at + 48, 8), 8), :] = skin
                if k + 1 < STEPS:
                    IS[k + 1, v, a : a + 1, :] = jnp.where(is_outer, top[0:1], edge[7:8])
                    WS[k + 1, v, a : a + 1, :] = edge[7:8]
                    if a == AZL - 1:
                        send_layers(k + 1, v)
            if k + 1 < STEPS:
                send_rest(k + 1, v)
            for hear, tell, when in (((None, 0, 0),), ((0, 1, 0), (1, 2, NV - 1)), ((2, 3, 4),))[k]:

                @pl.when(v == when)
                def _(hear=hear, tell=tell):
                    if hear is not None:
                        hear_word(hear)
                    pass_word(tell)

            return products([(k, k, 16 * k), (k, k + 1, 16 * k + 8)], v, moments)

        return body

    def products(which, v, moments):
        k = which[0][0]
        base = v * BLK
        sums = [[jnp.zeros((8, 128), F32) for _ in range(NV)] for _ in which]
        for p in range(BLK // 8):
            here = pl.ds(pl.multiple_of(base + p * 8, 8), 8)
            mine = [X[j, here, :] for _, j, _ in which]
            if p % 7 == 6:
                mine = [m * share for m in mine]
            for w in range(NV):
                other = X[k, w * BLK + p * 8 : w * BLK + p * 8 + 8, :]
                for q in range(len(which)):
                    sums[q][w] += other * mine[q]
        for q, (_, _, at) in enumerate(which):
            for w in range(NV):
                ACC[64 * q + w * 8 : 64 * q + w * 8 + 8, :] = sums[q][w]
            total = ACC[pl.ds(64 * q, 8, stride=8), :]
            for s in range(1, 8):
                total += ACC[pl.ds(64 * q + s, 8, stride=8), :]
            total = jnp.sum(total, axis=1, keepdims=True)
            moments = jnp.where(lane == at + v, total, moments)
        return moments

    def sum_copy(stage, d):
        at = place_in(stage)
        return pltpu.make_async_remote_copy(
            RX.at[stage, at], RX.at[stage, at], sum_send.at[stage], sum_recv.at[stage],
            device_id=peer(stage, d)[1], device_id_type=MESH,
        )

    def sum_all(stage):
        n = slots[stage] - 1
        block = RX.at[stage, pl.ds(0, n)]
        return pltpu.make_async_remote_copy(
            block, block, sum_send.at[stage], sum_recv.at[stage],
            device_id=peer(stage, 1)[1], device_id_type=MESH,
        )

    def sum_start(stage, value):
        RX[stage, place_in(stage)] = value
        for d in range(1, slots[stage]):
            sum_copy(stage, d).start()

    def sum_finish(stage):
        sum_all(stage).wait_recv()
        terms = [RX[stage, s] for s in range(slots[stage])]
        while len(terms) > 1:
            terms = [terms[q] + terms[q + 1] for q in range(0, len(terms), 2)]
        return terms[0]

    def prepare(r, c):
        for half in range(2):
            cols = [
                jnp.concatenate(
                    [X[k, pl.ds((2 * half + b) * ROWS + r, NV, stride=BLK), :] for k in range(4)], axis=0
                )
                for b in range(2)
            ]
            wide = jnp.concatenate(cols, axis=1)
            high = rounded(wide)
            T[2 * r + half] = jnp.concatenate([high, wide - high, high], axis=0).astype(BF16)
        return c

    zero8 = jnp.zeros((8, 128), F32)
    moments = zero8
    for k in range(STEPS):
        moments = lax.fori_loop(0, NV, apply(k), moments)
    sum_start(2, moments)
    hear_word(3)
    pl.semaphore_signal(word.at[4, 0], inc=1, device_id=to_half, device_id_type=MESH)
    sum_start(0, sum_finish(2))
    lax.fori_loop(0, 27, prepare, 0, unroll=3)
    for k in range(STEPS):
        sent(k)
    pl.semaphore_wait(word.at[4, 0], 1)
    sum_start(1, sum_finish(0))
    lax.fori_loop(27, 54, prepare, 0, unroll=3)
    for stage in (2, 0):
        sum_all(stage).wait_send()
    gram = sum_finish(1)

    shifted = pltpu.roll(gram, 120, axis=1) + THETA * gram
    table = []
    for i in range(STEPS):
        left_part = shifted if i == 0 else pltpu.roll(shifted, 128 - 8 * i, axis=1)
        right_part = pltpu.roll(gram, 24 - 8 * i, axis=1)
        table.append(jnp.where(lane < 24, left_part, jnp.where(lane < 32, right_part, 0.0)))
    full = (8, 128)

    def over(part):
        return jnp.broadcast_to(part, full)

    for at in range(STEPS):
        columns = [[over(t[:, 8 * at + q : 8 * at + q + 1]) for t in table] for q in range(8)]
        for r in range(8):
            inverse = 1.0 / over(columns[r][at][r : r + 1, :])
            scaled = over(table[at][r : r + 1, :]) * inverse
            ratios = {q: over(columns[q][at][r : r + 1, :]) * inverse for q in range(r + 1, 8)}
            for i in range(STEPS):
                for q, ratio in ratios.items():
                    reduced = columns[q][i] - columns[r][i] * ratio
                    columns[q][i] = jnp.where(row == r, ratio, reduced) if i == at else reduced
                reduced = table[i] - columns[r][i] * scaled
                table[i] = jnp.where(row == r, scaled, reduced) if i == at else reduced

    y = [jnp.where(lane < 8, pltpu.roll(t, 104, axis=1), 0.0) for t in table]
    eye = jnp.where(lane == row, 1.0, 0.0)
    into = [
        eye - THETA * y[0],
        -(y[0] + THETA * y[1]),
        -(y[1] + THETA * y[2]),
        -y[2],
    ]
    parts = [(y[k] if k < STEPS else zero8) + pltpu.roll(into[k], 8, axis=1) for k in range(4)]
    square = jnp.concatenate(parts + [jnp.zeros((96, 128), F32)], axis=0)
    mix = square.T[0:16, :]
    high = rounded(mix)
    MIX[...] = high + pltpu.roll(high, 32, axis=1) + pltpu.roll(mix - high, 64, axis=1)
    sum_all(1).wait_send()


PIECES = 4


def finish_kernel(T, MIX, sol_c, res_c, sol_s, res_s, o_sc, o_rc, o_ss, o_rs, sem):
    mix = MIX[...].astype(BF16)[:, 0:96]

    def rows_of(first, rows, o_sol, o_res):
        def body(r, c):
            for a in (0, 2):
                out = jnp.dot(mix, T[2 * (first + r) + a // 2], preferred_element_type=F32)
                for b in range(2):
                    here = pl.ds(r * AZL + a + b, NV, stride=rows * AZL)
                    o_sol[here, :] = out[0:8, b * 128 : b * 128 + 128]
                    o_res[here, :] = out[8:16, b * 128 : b * 128 + 128]
            return c

        return body

    def piece(i, o, dst, slot, rows):
        copies = []
        for v in range(NV):
            here = pl.ds(v * RC * AZL + i * rows, rows)
            copies.append(pltpu.make_async_copy(o.at[here, :], dst.at[here, :], sem.at[slot]))
        return copies

    each = RC // PIECES
    lax.fori_loop(0, RS, rows_of(RC, RS, o_ss, o_rs), 0, unroll=True)
    small = [
        pltpu.make_async_copy(o_ss, sol_s, sem.at[2]),
        pltpu.make_async_copy(o_rs, res_s, sem.at[3]),
    ]
    for copy in small:
        copy.start()
    for i in range(PIECES):
        lax.fori_loop(i * each, (i + 1) * each, rows_of(0, RC, o_sc, o_rc), 0, unroll=True)
        for copy in piece(i, o_sc, sol_c, 0, each * AZL) + piece(i, o_rc, res_c, 1, each * AZL):
            copy.start()
    for copy in small:
        copy.wait()
    pltpu.make_async_copy(o_sc, sol_c, sem.at[0]).wait()
    pltpu.make_async_copy(o_rc, res_c, sem.at[1]).wait()


def per_device(cavity_block, shell_block, column_matrix, shell_matrix, shifted_diagonal, shell_diagonal, wet_area):
    nc, ns = NV * RC * AZL, NV * RS * AZL
    anywhere = pl.BlockSpec(memory_space=pl.ANY)
    args = (
        cavity_block.reshape(nc, 128),
        shell_block.reshape(ns, 128),
        column_matrix.reshape(RC, RC),
        shell_matrix,
        shifted_diagonal.reshape(RC * AZL, 128),
        shell_diagonal.reshape(RS * AZL, 128),
        wet_area,
    )
    args = [pltpu.with_memory_space_constraint(x, pltpu.HBM) for x in args]
    inside = pl.BlockSpec(memory_space=pltpu.VMEM)
    basis, mix = pl.pallas_call(
        kernel,
        out_shape=(pltpu.VMEM((2 * (RC + RS), 96, 256), BF16), pltpu.VMEM((16, 128), F32)),
        in_specs=[anywhere] * 7,
        out_specs=(inside, inside),
        scratch_shapes=[
            pltpu.VMEM((4, NV * BLK, 128), F32),
            pltpu.VMEM((STEPS, NV, ROWS, 128), F32),
            pltpu.VMEM((STEPS, NV, ROWS, 128), F32),
            pltpu.VMEM((STEPS, NV, BLK, 128), F32),
            pltpu.VMEM((STEPS, NV, AZL, 128), F32),
            pltpu.VMEM((STEPS, NV, AZL, 128), F32),
            pltpu.VMEM((STEPS, NV, AZL, 128), F32),
            pltpu.VMEM((STEPS, NV, AZL, 128), F32),
            pltpu.VMEM((AZL, ROWS, 128), F32),
            pltpu.VMEM((64, 256), BF16),
            pltpu.VMEM((64, 128), F32),
            pltpu.VMEM((128, 128), F32),
            pltpu.VMEM((3, 16, 8, 128), F32),
            pltpu.VMEM((nc, 128), F32),
            pltpu.VMEM((ns, 128), F32),
            pltpu.VMEM((RC * AZL, 128), F32),
            pltpu.VMEM((RS * AZL, 128), F32),
            pltpu.VMEM((AZL, 128), F32),
            pltpu.VMEM((RC, RC), F32),
            pltpu.VMEM((RS, RS), F32),
            pltpu.SemaphoreType.DMA((6,)),
            pltpu.SemaphoreType.DMA((NV,)),
            pltpu.SemaphoreType.DMA((STEPS, 5)),
            pltpu.SemaphoreType.DMA((STEPS, NV, 5)),
            pltpu.SemaphoreType.DMA((3,)),
            pltpu.SemaphoreType.DMA((3,)),
            pltpu.SemaphoreType.REGULAR((5, 2)),
        ],
        compiler_params=pltpu.CompilerParams(
            collective_id=0, has_side_effects=True, vmem_limit_bytes=22 * 1024 * 1024
        ),
        name="block_cg",
    )(*args)
    outs = pl.pallas_call(
        finish_kernel,
        out_shape=(
            jax.ShapeDtypeStruct((nc, 128), F32),
            jax.ShapeDtypeStruct((nc, 128), F32),
            jax.ShapeDtypeStruct((ns, 128), F32),
            jax.ShapeDtypeStruct((ns, 128), F32),
        ),
        in_specs=[inside, inside],
        out_specs=(anywhere,) * 4,
        scratch_shapes=[
            pltpu.VMEM((nc, 128), F32),
            pltpu.VMEM((nc, 128), F32),
            pltpu.VMEM((ns, 128), F32),
            pltpu.VMEM((ns, 128), F32),
            pltpu.SemaphoreType.DMA((4,)),
        ],
        compiler_params=pltpu.CompilerParams(vmem_limit_bytes=22 * 1024 * 1024),
        name="combine_basis",
    )(
        pltpu.with_memory_space_constraint(basis, pltpu.VMEM),
        pltpu.with_memory_space_constraint(mix, pltpu.VMEM),
    )
    return (
        outs[0].reshape(NV, RC, AZL, 128),
        outs[1].reshape(NV, RC, AZL, 128),
        outs[2].reshape(NV, RS, AZL, 128),
        outs[3].reshape(NV, RS, AZL, 128),
    )


def solution(mesh):
    return jax.shard_map(
        per_device,
        mesh=mesh,
        in_specs=(
            P(None, "grp", "az", "ax"),
            P(None, None, "az", "ax"),
            P("grp", None, None),
            P(),
            P("grp", "az", "ax"),
            P(None, "az", "ax"),
            P("az", "ax"),
        ),
        out_specs=(
            P(None, "grp", "az", "ax"),
            P(None, "grp", "az", "ax"),
            P(None, None, "az", "ax"),
            P(None, None, "az", "ax"),
        ),
        check_vma=False,
    )
```

```python
import jax
import jax.numpy as jnp
from jax import lax
from jax.experimental import pallas as pl
from jax.experimental.pallas import tpu as pltpu
from jax.sharding import PartitionSpec as P

NV = 8
RC = 48
RS = 6
ROWS = 56
LAYER = RC + RS
AZL = 4
BLK = AZL * ROWS
STEPS = 3
THETA = 9.0
MESH = pl.DeviceIdType.MESH
F32 = jnp.float32
BF16 = jnp.bfloat16


def rounded(value):
    return value.astype(BF16).astype(F32)


def kernel(
    cav, shl, colm, shm, dia, sdia, wet,
    T, MIX,
    X, HL, HR, SB, IS, IR, WS, WR, DG, W, STG, ACC, RX,
    raw_c, raw_s, raw_d, raw_sd, raw_w, raw_cm, raw_sm,
    in_sem, vec_sem, send_sem, recv_sem, sum_send, sum_recv, word,
):
    grp = lax.axis_index("grp")
    az = lax.axis_index("az")
    ax = lax.axis_index("ax")
    naz = 64
    right = lax.rem(az + 1, naz)
    left = lax.rem(az + naz - 1, naz)
    px = az // 16
    pz = lax.rem(az // 4, 4)
    py = lax.rem(az, 4)

    barrier = pltpu.get_barrier_semaphore()

    def hello(where):
        pl.semaphore_signal(barrier, inc=1, device_id=where, device_id_type=MESH)

    here1 = px * 4 + py
    here2 = grp * 4 + pz
    slots = (16, 8, 2)

    def place_in(stage):
        return (here1, here2, ax)[stage]

    def peer(stage, d):
        if stage == 0:
            x, y = lax.rem(px + d // 4, 4), lax.rem(py + d % 4, 4)
            return x * 4 + y, {"grp": grp, "az": x * 16 + pz * 4 + y, "ax": ax}
        if stage == 1:
            g, z = lax.rem(grp + d // 4, 2), lax.rem(pz + d % 4, 4)
            return g * 4 + z, {"grp": g, "az": px * 16 + z * 4 + py, "ax": ax}
        return 1 - ax, {"grp": grp, "az": az, "ax": 1 - ax}

    def far(step, side):
        apart = 2 ** (step + 1)
        return {"grp": grp, "az": lax.rem(az + (apart if side == 0 else naz - apart), naz), "ax": ax}

    def pass_word(step):
        for side in range(2):
            pl.semaphore_signal(word.at[step, side], inc=1, device_id=far(step, side), device_id_type=MESH)

    def hear_word(step):
        for side in range(2):
            pl.semaphore_wait(word.at[step, side], 1)

    to_right = {"grp": grp, "az": right, "ax": ax}
    to_left = {"grp": grp, "az": left, "ax": ax}
    to_core = {"grp": grp, "az": az, "ax": 1 - ax}
    to_half = {"grp": 1 - grp, "az": az, "ax": ax}
    for where in (to_right, to_left, to_core, to_half):
        hello(where)

    loads = [
        pltpu.make_async_copy(src, dst, in_sem.at[i])
        for i, (src, dst) in enumerate(
            [(shl, raw_s), (dia, raw_d), (sdia, raw_sd), (wet, raw_w), (colm, raw_cm), (shm, raw_sm)]
        )
    ]
    def load_vector(v):
        here = pl.ds(pl.multiple_of(v * (RC * AZL), 8), RC * AZL)
        return pltpu.make_async_copy(cav.at[here, :], raw_c.at[here, :], vec_sem.at[v])

    loads[0].start()
    for v in range(NV):
        load_vector(v).start()
    for load in loads[1:]:
        load.start()

    outer = (grp == 1).astype(F32)
    is_outer = grp == 1
    lane = lax.broadcasted_iota(jnp.int32, (8, 128), 1)
    row = lax.broadcasted_iota(jnp.int32, (8, 128), 0)

    def rows_to_send(k, v):
        for a in range(AZL):
            at = v * BLK + a * ROWS
            first = X[k, pl.ds(pl.multiple_of(at, 8), 8), :][0:1]
            last = X[k, pl.ds(pl.multiple_of(at + 40, 8), 8), :][7:8]
            IS[k, v, a : a + 1, :] = jnp.where(is_outer, first, last)
            WS[k, v, a : a + 1, :] = last

    def exchange(k, v):
        base = pl.multiple_of(v * BLK, 8)
        top = pl.multiple_of(v * BLK + 3 * ROWS, 8)
        return (
            pltpu.make_async_remote_copy(
                X.at[k, pl.ds(top, LAYER), :], HL.at[k, v, pl.ds(0, LAYER), :], send_sem.at[k, 0], recv_sem.at[k, v, 0],
                device_id=to_right, device_id_type=MESH,
            ),
            pltpu.make_async_remote_copy(
                X.at[k, pl.ds(base, LAYER), :], HR.at[k, v, pl.ds(0, LAYER), :], send_sem.at[k, 1], recv_sem.at[k, v, 1],
                device_id=to_left, device_id_type=MESH,
            ),
            pltpu.make_async_remote_copy(
                X.at[k, pl.ds(base, BLK), :], SB.at[k, v], send_sem.at[k, 2], recv_sem.at[k, v, 2],
                device_id=to_core, device_id_type=MESH,
            ),
            pltpu.make_async_remote_copy(
                IS.at[k, v], IR.at[k, v], send_sem.at[k, 3], recv_sem.at[k, v, 3],
                device_id=to_half, device_id_type=MESH,
            ),
        )

    def wall_copy(k, v):
        return pltpu.make_async_remote_copy(
            WS.at[k, v], WR.at[k, v], send_sem.at[k, 4], recv_sem.at[k, v, 4], device_id=to_half, device_id_type=MESH
        )

    def send_layers(k, v):
        for copy in exchange(k, v)[:2]:
            copy.start()

    def send_rest(k, v):
        for copy in exchange(k, v)[2:]:
            copy.start()

        @pl.when(is_outer)
        def _():
            wall_copy(k, v).start()

    def sent(k):
        def all_of(i, buf, where):
            pltpu.make_async_remote_copy(
                buf.at[k], buf.at[k], send_sem.at[k, i], recv_sem.at[k, 0, i], device_id=where, device_id_type=MESH
            ).wait_send()

        for i, (buf, where) in enumerate(((HL, to_right), (HR, to_left), (SB, to_core), (IS, to_half))):
            part = LAYER if i < 2 else buf.shape[2]
            all_of(i, buf.at[:, :, pl.ds(0, part), :], where)

        @pl.when(is_outer)
        def _():
            all_of(4, WS, to_half)

    loads[0].wait()

    def settle(v, c):
        load_vector(v).wait()
        for a in range(AZL):
            at = v * BLK + a * ROWS
            X[0, pl.ds(pl.multiple_of(at, 8), RC), :] = raw_c[pl.ds(v * (RC * AZL) + a, RC, stride=AZL), :]
            tail = jnp.concatenate(
                [raw_s[pl.ds(v * (RS * AZL) + a, RS, stride=AZL), :], jnp.zeros((2, 128), F32)], axis=0
            )
            X[0, pl.ds(pl.multiple_of(at + RC, 8), 8), :] = tail
        rows_to_send(0, v)
        for k in range(STEPS):
            HL[k, v, LAYER:ROWS, :] = jnp.zeros((ROWS - LAYER, 128), F32)
            HR[k, v, LAYER:ROWS, :] = jnp.zeros((ROWS - LAYER, 128), F32)
        return c

    lax.fori_loop(0, NV, settle, 0)

    def first_send(v, c):
        send_layers(0, v)
        send_rest(0, v)
        return c

    pl.semaphore_wait(barrier, 4)
    lax.fori_loop(0, NV, first_send, 0)
    for load in loads[1:]:
        load.wait()

    for a in range(AZL):
        DG[a, 0:RC, :] = raw_d[pl.ds(a, RC, stride=AZL), :] + (4.0 - THETA)
        DG[a, RC:ROWS, :] = jnp.concatenate(
            [raw_sd[pl.ds(a, RS, stride=AZL), :] + (4.0 - THETA), jnp.zeros((2, 128), F32)], axis=0
        )
    STG[...] = jnp.zeros((64, 128), F32)
    STG[56:62, 0:RS] = raw_sm[...]
    shell_rows = pltpu.roll(STG[56:64, :], RC, axis=1)
    STG[56:64, :] = jnp.zeros((8, 128), F32)
    STG[0:RC, 0:RC] = raw_cm[...]
    STG[RC:ROWS, :] = shell_rows
    row64 = lax.broadcasted_iota(jnp.int32, (64, 128), 0)
    lane64 = lax.broadcasted_iota(jnp.int32, (64, 128), 1)
    matrix = STG[...]
    matrix = jnp.where((lane64 == 58) & (row64 == RC - 1), -outer, matrix)
    high = rounded(matrix)
    W[...] = jnp.concatenate([high + pltpu.roll(high, 64, axis=1), matrix - high], axis=1).astype(BF16)

    lane56 = lax.broadcasted_iota(jnp.int32, (ROWS, 128), 1)
    first_lane = lane56 == 0
    last_lane = lane56 == 127
    from_left = (ax == 1).astype(F32)
    from_right = (ax == 0).astype(F32)
    share = 1.0 - outer

    def apply(k):
        def body(v, moments):
            base = v * BLK
            from_left_slab, from_right_slab, from_core, from_half = exchange(k, v)
            from_core.wait_recv()
            own = [X[k, pl.ds(pl.multiple_of(base + a * ROWS, 8), ROWS), :] for a in range(AZL)]
            wet_rows = [raw_w[a : a + 1, :] for a in range(AZL)]
            spread = []
            for a in range(AZL):
                extra = jnp.where(row == 2, wet_rows[a] * own[a][RC : RC + 1], 0.0)
                spread.append(jnp.concatenate([own[a], extra], axis=0))
            wide = jnp.concatenate(spread, axis=1)
            high = rounded(wide)
            stacked = jnp.concatenate([high, wide - high, high], axis=0).astype(BF16)
            mixed = jnp.dot(W[:, 0:192], stacked, preferred_element_type=F32)
            part = []
            for a in range(AZL):
                side = SB[k, v, a * ROWS : (a + 1) * ROWS, :]
                lower = pltpu.roll(jnp.where(last_lane, side * from_left, own[a]), 1, axis=1)
                upper = pltpu.roll(jnp.where(first_lane, side * from_right, own[a]), 127, axis=1)
                value = mixed[0:ROWS, a * 128 : (a + 1) * 128] + DG[a] * own[a] - (lower + upper)
                if a > 0:
                    value = value - own[a - 1]
                if a < AZL - 1:
                    value = value - own[a + 1]
                part.append(value)

            from_left_slab.wait_recv()
            from_right_slab.wait_recv()
            from_half.wait_recv()

            @pl.when(grp == 0)
            def _():
                wall_copy(k, v).wait_recv()

            got, far = IR[k, v], WR[k, v]
            for a in (0, AZL - 1, *range(1, AZL - 1)):
                value = part[a]
                if a == 0:
                    value = value - HL[k, v]
                if a == AZL - 1:
                    value = value - HR[k, v]
                wall = jnp.where(is_outer, own[a][RC - 1 : RC], far[a : a + 1])
                at = base + a * ROWS
                top = value[0:8] - jnp.where(row == 0, outer * got[a : a + 1], 0.0)
                edge = value[40:48] - jnp.where(row == 7, share * got[a : a + 1], 0.0)
                skin = value[48:56] - jnp.where(row == 0, wet_rows[a] * wall, 0.0)
                X[k + 1, pl.ds(pl.multiple_of(at, 8), 8), :] = top
                X[k + 1, pl.ds(pl.multiple_of(at + 8, 8), 32), :] = value[8:40]
                X[k + 1, pl.ds(pl.multiple_of(at + 40, 8), 8), :] = edge
                X[k + 1, pl.ds(pl.multiple_of(at + 48, 8), 8), :] = skin
                if k + 1 < STEPS:
                    IS[k + 1, v, a : a + 1, :] = jnp.where(is_outer, top[0:1], edge[7:8])
                    WS[k + 1, v, a : a + 1, :] = edge[7:8]
                    if a == AZL - 1:
                        send_layers(k + 1, v)
            if k + 1 < STEPS:
                send_rest(k + 1, v)
            for hear, tell, when in (((None, 0, 0),), ((0, 1, 0), (1, 2, NV - 1)), ((2, 3, 4),))[k]:

                @pl.when(v == when)
                def _(hear=hear, tell=tell):
                    if hear is not None:
                        hear_word(hear)
                    pass_word(tell)

            return products([(k, k, 16 * k), (k, k + 1, 16 * k + 8)], v, moments)

        return body

    def products(which, v, moments):
        k = which[0][0]
        base = v * BLK
        sums = [[jnp.zeros((8, 128), F32) for _ in range(NV)] for _ in which]
        for p in range(BLK // 8):
            here = pl.ds(pl.multiple_of(base + p * 8, 8), 8)
            mine = [X[j, here, :] for _, j, _ in which]
            if p % 7 == 6:
                mine = [m * share for m in mine]
            for w in range(NV):
                other = X[k, w * BLK + p * 8 : w * BLK + p * 8 + 8, :]
                for q in range(len(which)):
                    sums[q][w] += other * mine[q]
        for q, (_, _, at) in enumerate(which):
            for w in range(NV):
                ACC[64 * q + w * 8 : 64 * q + w * 8 + 8, :] = sums[q][w]
            total = ACC[pl.ds(64 * q, 8, stride=8), :]
            for s in range(1, 8):
                total += ACC[pl.ds(64 * q + s, 8, stride=8), :]
            total = jnp.sum(total, axis=1, keepdims=True)
            moments = jnp.where(lane == at + v, total, moments)
        return moments

    def sum_copy(stage, d):
        at = place_in(stage)
        return pltpu.make_async_remote_copy(
            RX.at[stage, at], RX.at[stage, at], sum_send.at[stage], sum_recv.at[stage],
            device_id=peer(stage, d)[1], device_id_type=MESH,
        )

    def sum_all(stage):
        n = slots[stage] - 1
        block = RX.at[stage, pl.ds(0, n)]
        return pltpu.make_async_remote_copy(
            block, block, sum_send.at[stage], sum_recv.at[stage],
            device_id=peer(stage, 1)[1], device_id_type=MESH,
        )

    def hops(stage, d):
        major, minor = d // 4, d % 4
        return min(minor, 4 - minor) + (min(major, 4 - major) if stage == 0 else 4 * major)

    def sum_start(stage, value):
        RX[stage, place_in(stage)] = value
        for d in sorted(range(1, slots[stage]), key=lambda d: hops(stage, d), reverse=True):
            sum_copy(stage, d).start()

    def sum_finish(stage):
        sum_all(stage).wait_recv()
        terms = [RX[stage, s] for s in range(slots[stage])]
        while len(terms) > 1:
            terms = [terms[q] + terms[q + 1] for q in range(0, len(terms), 2)]
        return terms[0]

    def prepare(r, c):
        for half in range(2):
            cols = [
                jnp.concatenate(
                    [X[k, pl.ds((2 * half + b) * ROWS + r, NV, stride=BLK), :] for k in range(4)], axis=0
                )
                for b in range(2)
            ]
            wide = jnp.concatenate(cols, axis=1)
            high = rounded(wide)
            T[2 * r + half] = jnp.concatenate([high, wide - high, high], axis=0).astype(BF16)
        return c

    zero8 = jnp.zeros((8, 128), F32)
    moments = zero8
    for k in range(STEPS):
        moments = lax.fori_loop(0, NV, apply(k), moments)
    sum_start(2, moments)
    hear_word(3)
    pl.semaphore_signal(word.at[4, 0], inc=1, device_id=to_half, device_id_type=MESH)
    sum_start(0, sum_finish(2))
    lax.fori_loop(0, 27, prepare, 0, unroll=3)
    for k in range(STEPS):
        sent(k)
    pl.semaphore_wait(word.at[4, 0], 1)
    sum_start(1, sum_finish(0))
    lax.fori_loop(27, 54, prepare, 0, unroll=3)
    for stage in (2, 0):
        sum_all(stage).wait_send()
    gram = sum_finish(1)

    shifted = pltpu.roll(gram, 120, axis=1) + THETA * gram
    table = []
    for i in range(STEPS):
        left_part = shifted if i == 0 else pltpu.roll(shifted, 128 - 8 * i, axis=1)
        right_part = pltpu.roll(gram, 24 - 8 * i, axis=1)
        table.append(jnp.where(lane < 24, left_part, jnp.where(lane < 32, right_part, 0.0)))
    full = (8, 128)

    def over(part):
        return jnp.broadcast_to(part, full)

    for at in range(STEPS):
        columns = [[over(t[:, 8 * at + q : 8 * at + q + 1]) for t in table] for q in range(8)]
        for r in range(8):
            inverse = 1.0 / over(columns[r][at][r : r + 1, :])
            scaled = over(table[at][r : r + 1, :]) * inverse
            ratios = {q: over(columns[q][at][r : r + 1, :]) * inverse for q in range(r + 1, 8)}
            for i in range(STEPS):
                for q, ratio in ratios.items():
                    reduced = columns[q][i] - columns[r][i] * ratio
                    columns[q][i] = jnp.where(row == r, ratio, reduced) if i == at else reduced
                reduced = table[i] - columns[r][i] * scaled
                table[i] = jnp.where(row == r, scaled, reduced) if i == at else reduced

    y = [jnp.where(lane < 8, pltpu.roll(t, 104, axis=1), 0.0) for t in table]
    eye = jnp.where(lane == row, 1.0, 0.0)
    into = [
        eye - THETA * y[0],
        -(y[0] + THETA * y[1]),
        -(y[1] + THETA * y[2]),
        -y[2],
    ]
    parts = [(y[k] if k < STEPS else zero8) + pltpu.roll(into[k], 8, axis=1) for k in range(4)]
    square = jnp.concatenate(parts, axis=0)
    turned = square.T[0:16, :]
    mix = jnp.concatenate([turned, jnp.zeros((16, 96), F32)], axis=1)
    high = rounded(mix)
    MIX[...] = high + pltpu.roll(high, 32, axis=1) + pltpu.roll(mix - high, 64, axis=1)
    sum_all(1).wait_send()


PIECES = 4


def finish_kernel(T, MIX, sol_c, res_c, sol_s, res_s, o_sc, o_rc, o_ss, o_rs, sem):
    mix = MIX[...].astype(BF16)[:, 0:96]

    def rows_of(first, rows, o_sol, o_res):
        def body(r, c):
            for a in (0, 2):
                out = jnp.dot(mix, T[2 * (first + r) + a // 2], preferred_element_type=F32)
                for b in range(2):
                    here = pl.ds(r * AZL + a + b, NV, stride=rows * AZL)
                    o_sol[here, :] = out[0:8, b * 128 : b * 128 + 128]
                    o_res[here, :] = out[8:16, b * 128 : b * 128 + 128]
            return c

        return body

    def piece(i, o, dst, slot, rows):
        copies = []
        for v in range(NV):
            here = pl.ds(v * RC * AZL + i * rows, rows)
            copies.append(pltpu.make_async_copy(o.at[here, :], dst.at[here, :], sem.at[slot]))
        return copies

    each = RC // PIECES
    lax.fori_loop(0, RS, rows_of(RC, RS, o_ss, o_rs), 0, unroll=True)
    small = [
        pltpu.make_async_copy(o_ss, sol_s, sem.at[2]),
        pltpu.make_async_copy(o_rs, res_s, sem.at[3]),
    ]
    for copy in small:
        copy.start()
    for i in range(PIECES):
        lax.fori_loop(i * each, (i + 1) * each, rows_of(0, RC, o_sc, o_rc), 0, unroll=True)
        for copy in piece(i, o_sc, sol_c, 0, each * AZL) + piece(i, o_rc, res_c, 1, each * AZL):
            copy.start()
    for copy in small:
        copy.wait()
    pltpu.make_async_copy(o_sc, sol_c, sem.at[0]).wait()
    pltpu.make_async_copy(o_rc, res_c, sem.at[1]).wait()


def per_device(cavity_block, shell_block, column_matrix, shell_matrix, shifted_diagonal, shell_diagonal, wet_area):
    nc, ns = NV * RC * AZL, NV * RS * AZL
    anywhere = pl.BlockSpec(memory_space=pl.ANY)
    args = (
        cavity_block.reshape(nc, 128),
        shell_block.reshape(ns, 128),
        column_matrix.reshape(RC, RC),
        shell_matrix,
        shifted_diagonal.reshape(RC * AZL, 128),
        shell_diagonal.reshape(RS * AZL, 128),
        wet_area,
    )
    args = [pltpu.with_memory_space_constraint(x, pltpu.HBM) for x in args]
    inside = pl.BlockSpec(memory_space=pltpu.VMEM)
    basis, mix = pl.pallas_call(
        kernel,
        out_shape=(pltpu.VMEM((2 * (RC + RS), 96, 256), BF16), pltpu.VMEM((16, 128), F32)),
        in_specs=[anywhere] * 7,
        out_specs=(inside, inside),
        scratch_shapes=[
            pltpu.VMEM((4, NV * BLK, 128), F32),
            pltpu.VMEM((STEPS, NV, ROWS, 128), F32),
            pltpu.VMEM((STEPS, NV, ROWS, 128), F32),
            pltpu.VMEM((STEPS, NV, BLK, 128), F32),
            pltpu.VMEM((STEPS, NV, AZL, 128), F32),
            pltpu.VMEM((STEPS, NV, AZL, 128), F32),
            pltpu.VMEM((STEPS, NV, AZL, 128), F32),
            pltpu.VMEM((STEPS, NV, AZL, 128), F32),
            pltpu.VMEM((AZL, ROWS, 128), F32),
            pltpu.VMEM((64, 256), BF16),
            pltpu.VMEM((64, 128), F32),
            pltpu.VMEM((128, 128), F32),
            pltpu.VMEM((3, 16, 8, 128), F32),
            pltpu.VMEM((nc, 128), F32),
            pltpu.VMEM((ns, 128), F32),
            pltpu.VMEM((RC * AZL, 128), F32),
            pltpu.VMEM((RS * AZL, 128), F32),
            pltpu.VMEM((AZL, 128), F32),
            pltpu.VMEM((RC, RC), F32),
            pltpu.VMEM((RS, RS), F32),
            pltpu.SemaphoreType.DMA((6,)),
            pltpu.SemaphoreType.DMA((NV,)),
            pltpu.SemaphoreType.DMA((STEPS, 5)),
            pltpu.SemaphoreType.DMA((STEPS, NV, 5)),
            pltpu.SemaphoreType.DMA((3,)),
            pltpu.SemaphoreType.DMA((3,)),
            pltpu.SemaphoreType.REGULAR((5, 2)),
        ],
        compiler_params=pltpu.CompilerParams(
            collective_id=0, has_side_effects=True, vmem_limit_bytes=22 * 1024 * 1024
        ),
        name="block_cg",
    )(*args)
    outs = pl.pallas_call(
        finish_kernel,
        out_shape=(
            jax.ShapeDtypeStruct((nc, 128), F32),
            jax.ShapeDtypeStruct((nc, 128), F32),
            jax.ShapeDtypeStruct((ns, 128), F32),
            jax.ShapeDtypeStruct((ns, 128), F32),
        ),
        in_specs=[inside, inside],
        out_specs=(anywhere,) * 4,
        scratch_shapes=[
            pltpu.VMEM((nc, 128), F32),
            pltpu.VMEM((nc, 128), F32),
            pltpu.VMEM((ns, 128), F32),
            pltpu.VMEM((ns, 128), F32),
            pltpu.SemaphoreType.DMA((4,)),
        ],
        compiler_params=pltpu.CompilerParams(vmem_limit_bytes=22 * 1024 * 1024),
        name="combine_basis",
    )(
        pltpu.with_memory_space_constraint(basis, pltpu.VMEM),
        pltpu.with_memory_space_constraint(mix, pltpu.VMEM),
    )
    return (
        outs[0].reshape(NV, RC, AZL, 128),
        outs[1].reshape(NV, RC, AZL, 128),
        outs[2].reshape(NV, RS, AZL, 128),
        outs[3].reshape(NV, RS, AZL, 128),
    )


def solution(mesh):
    return jax.shard_map(
        per_device,
        mesh=mesh,
        in_specs=(
            P(None, "grp", "az", "ax"),
            P(None, None, "az", "ax"),
            P("grp", None, None),
            P(),
            P("grp", "az", "ax"),
            P(None, "az", "ax"),
            P("az", "ax"),
        ),
        out_specs=(
            P(None, "grp", "az", "ax"),
            P(None, "grp", "az", "ax"),
            P(None, None, "az", "ax"),
            P(None, None, "az", "ax"),
        ),
        check_vma=False,
    )
```

```python
import jax
import jax.numpy as jnp
from jax import lax
from jax.experimental import pallas as pl
from jax.experimental.pallas import tpu as pltpu
from jax.sharding import PartitionSpec as P

NV = 8
RC = 48
RS = 6
ROWS = 56
LAYER = RC + RS
AZL = 4
BLK = AZL * ROWS
STEPS = 3
THETA = 9.0
MESH = pl.DeviceIdType.MESH
F32 = jnp.float32
BF16 = jnp.bfloat16


def rounded(value):
    return value.astype(BF16).astype(F32)


def kernel(
    cav, shl, colm, shm, dia, sdia, wet,
    T, MIX,
    X, HL, HR, SB, IS, IR, WS, WR, DG, W, STG, ACC, RX,
    raw_c, raw_s, raw_d, raw_sd, raw_w, raw_cm, raw_sm,
    in_sem, vec_sem, send_sem, recv_sem, sum_send, sum_recv, word,
):
    grp = lax.axis_index("grp")
    az = lax.axis_index("az")
    ax = lax.axis_index("ax")
    naz = 64
    right = lax.rem(az + 1, naz)
    left = lax.rem(az + naz - 1, naz)
    px = az // 16
    pz = lax.rem(az // 4, 4)
    py = lax.rem(az, 4)

    barrier = pltpu.get_barrier_semaphore()

    def hello(where):
        pl.semaphore_signal(barrier, inc=1, device_id=where, device_id_type=MESH)

    here1 = px * 4 + py
    here2 = grp * 4 + pz
    slots = (16, 8, 2)

    def place_in(stage):
        return (here1, here2, ax)[stage]

    def peer(stage, d):
        if stage == 0:
            x, y = lax.rem(px + d // 4, 4), lax.rem(py + d % 4, 4)
            return x * 4 + y, {"grp": grp, "az": x * 16 + pz * 4 + y, "ax": ax}
        if stage == 1:
            g, z = lax.rem(grp + d // 4, 2), lax.rem(pz + d % 4, 4)
            return g * 4 + z, {"grp": g, "az": px * 16 + z * 4 + py, "ax": ax}
        return 1 - ax, {"grp": grp, "az": az, "ax": 1 - ax}

    def far(step, side):
        apart = 2 ** (step + 1)
        return {"grp": grp, "az": lax.rem(az + (apart if side == 0 else naz - apart), naz), "ax": ax}

    def pass_word(step):
        for side in range(2):
            pl.semaphore_signal(word.at[step, side], inc=1, device_id=far(step, side), device_id_type=MESH)

    def hear_word(step):
        for side in range(2):
            pl.semaphore_wait(word.at[step, side], 1)

    to_right = {"grp": grp, "az": right, "ax": ax}
    to_left = {"grp": grp, "az": left, "ax": ax}
    to_core = {"grp": grp, "az": az, "ax": 1 - ax}
    to_half = {"grp": 1 - grp, "az": az, "ax": ax}
    for where in (to_right, to_left, to_core, to_half):
        hello(where)

    loads = [
        pltpu.make_async_copy(src, dst, in_sem.at[i])
        for i, (src, dst) in enumerate(
            [(shl, raw_s), (dia, raw_d), (sdia, raw_sd), (wet, raw_w), (colm, raw_cm), (shm, raw_sm)]
        )
    ]
    def load_vector(v):
        here = pl.ds(pl.multiple_of(v * (RC * AZL), 8), RC * AZL)
        return pltpu.make_async_copy(cav.at[here, :], raw_c.at[here, :], vec_sem.at[v])

    loads[0].start()
    for v in range(NV):
        load_vector(v).start()
    for load in loads[1:]:
        load.start()

    outer = (grp == 1).astype(F32)
    is_outer = grp == 1
    lane = lax.broadcasted_iota(jnp.int32, (8, 128), 1)
    row = lax.broadcasted_iota(jnp.int32, (8, 128), 0)

    def rows_to_send(k, v):
        for a in range(AZL):
            at = v * BLK + a * ROWS
            first = X[k, pl.ds(pl.multiple_of(at, 8), 8), :][0:1]
            last = X[k, pl.ds(pl.multiple_of(at + 40, 8), 8), :][7:8]
            IS[k, v, a : a + 1, :] = jnp.where(is_outer, first, last)
            WS[k, v, a : a + 1, :] = last

    def exchange(k, v):
        base = pl.multiple_of(v * BLK, 8)
        top = pl.multiple_of(v * BLK + 3 * ROWS, 8)
        return (
            pltpu.make_async_remote_copy(
                X.at[k, pl.ds(top, LAYER), :], HL.at[k, v, pl.ds(0, LAYER), :], send_sem.at[k, 0], recv_sem.at[k, v, 0],
                device_id=to_right, device_id_type=MESH,
            ),
            pltpu.make_async_remote_copy(
                X.at[k, pl.ds(base, LAYER), :], HR.at[k, v, pl.ds(0, LAYER), :], send_sem.at[k, 1], recv_sem.at[k, v, 1],
                device_id=to_left, device_id_type=MESH,
            ),
            pltpu.make_async_remote_copy(
                X.at[k, pl.ds(base, BLK), :], SB.at[k, v], send_sem.at[k, 2], recv_sem.at[k, v, 2],
                device_id=to_core, device_id_type=MESH,
            ),
            pltpu.make_async_remote_copy(
                IS.at[k, v], IR.at[k, v], send_sem.at[k, 3], recv_sem.at[k, v, 3],
                device_id=to_half, device_id_type=MESH,
            ),
        )

    def wall_copy(k, v):
        return pltpu.make_async_remote_copy(
            WS.at[k, v], WR.at[k, v], send_sem.at[k, 4], recv_sem.at[k, v, 4], device_id=to_half, device_id_type=MESH
        )

    def send_layers(k, v):
        for copy in exchange(k, v)[:2]:
            copy.start()

    def send_rest(k, v):
        for copy in exchange(k, v)[2:]:
            copy.start()

        @pl.when(is_outer)
        def _():
            wall_copy(k, v).start()

    def sent(k):
        def all_of(i, buf, where):
            pltpu.make_async_remote_copy(
                buf.at[k], buf.at[k], send_sem.at[k, i], recv_sem.at[k, 0, i], device_id=where, device_id_type=MESH
            ).wait_send()

        for i, (buf, where) in enumerate(((HL, to_right), (HR, to_left), (SB, to_core), (IS, to_half))):
            part = LAYER if i < 2 else buf.shape[2]
            all_of(i, buf.at[:, :, pl.ds(0, part), :], where)

        @pl.when(is_outer)
        def _():
            all_of(4, WS, to_half)

    loads[0].wait()

    def settle(v, c):
        load_vector(v).wait()
        for a in range(AZL):
            at = v * BLK + a * ROWS
            X[0, pl.ds(pl.multiple_of(at, 8), RC), :] = raw_c[pl.ds(v * (RC * AZL) + a, RC, stride=AZL), :]
            tail = jnp.concatenate(
                [raw_s[pl.ds(v * (RS * AZL) + a, RS, stride=AZL), :], jnp.zeros((2, 128), F32)], axis=0
            )
            X[0, pl.ds(pl.multiple_of(at + RC, 8), 8), :] = tail
        rows_to_send(0, v)
        for k in range(STEPS):
            HL[k, v, LAYER:ROWS, :] = jnp.zeros((ROWS - LAYER, 128), F32)
            HR[k, v, LAYER:ROWS, :] = jnp.zeros((ROWS - LAYER, 128), F32)
        return c

    lax.fori_loop(0, NV, settle, 0)

    def first_send(v, c):
        send_layers(0, v)
        send_rest(0, v)
        return c

    pl.semaphore_wait(barrier, 4)
    lax.fori_loop(0, NV, first_send, 0)
    for load in loads[1:]:
        load.wait()

    for a in range(AZL):
        DG[a, 0:RC, :] = raw_d[pl.ds(a, RC, stride=AZL), :] + (4.0 - THETA)
        DG[a, RC:ROWS, :] = jnp.concatenate(
            [raw_sd[pl.ds(a, RS, stride=AZL), :] + (4.0 - THETA), jnp.zeros((2, 128), F32)], axis=0
        )
    STG[...] = jnp.zeros((64, 128), F32)
    STG[56:62, 0:RS] = raw_sm[...]
    shell_rows = pltpu.roll(STG[56:64, :], RC, axis=1)
    STG[56:64, :] = jnp.zeros((8, 128), F32)
    STG[0:RC, 0:RC] = raw_cm[...]
    STG[RC:ROWS, :] = shell_rows
    row64 = lax.broadcasted_iota(jnp.int32, (64, 128), 0)
    lane64 = lax.broadcasted_iota(jnp.int32, (64, 128), 1)
    matrix = STG[...]
    matrix = jnp.where((lane64 == 58) & (row64 == RC - 1), -outer, matrix)
    high = rounded(matrix)
    W[...] = jnp.concatenate([high + pltpu.roll(high, 64, axis=1), matrix - high], axis=1).astype(BF16)

    lane56 = lax.broadcasted_iota(jnp.int32, (ROWS, 128), 1)
    first_lane = lane56 == 0
    last_lane = lane56 == 127
    from_left = (ax == 1).astype(F32)
    from_right = (ax == 0).astype(F32)
    share = 1.0 - outer

    def apply(k):
        def body(v, moments):
            base = v * BLK
            from_left_slab, from_right_slab, from_core, from_half = exchange(k, v)
            from_core.wait_recv()
            own = [X[k, pl.ds(pl.multiple_of(base + a * ROWS, 8), ROWS), :] for a in range(AZL)]
            wet_rows = [raw_w[a : a + 1, :] for a in range(AZL)]
            spread = []
            for a in range(AZL):
                extra = jnp.where(row == 2, wet_rows[a] * own[a][RC : RC + 1], 0.0)
                spread.append(jnp.concatenate([own[a], extra], axis=0))
            wide = jnp.concatenate(spread, axis=1)
            high = rounded(wide)
            stacked = jnp.concatenate([high, wide - high, high], axis=0).astype(BF16)
            mixed = jnp.dot(W[:, 0:192], stacked, preferred_element_type=F32)
            part = []
            for a in range(AZL):
                side = SB[k, v, a * ROWS : (a + 1) * ROWS, :]
                lower = pltpu.roll(jnp.where(last_lane, side * from_left, own[a]), 1, axis=1)
                upper = pltpu.roll(jnp.where(first_lane, side * from_right, own[a]), 127, axis=1)
                value = mixed[0:ROWS, a * 128 : (a + 1) * 128] + DG[a] * own[a] - (lower + upper)
                if a > 0:
                    value = value - own[a - 1]
                if a < AZL - 1:
                    value = value - own[a + 1]
                part.append(value)

            from_left_slab.wait_recv()
            from_right_slab.wait_recv()
            from_half.wait_recv()

            @pl.when(grp == 0)
            def _():
                wall_copy(k, v).wait_recv()

            got, far = IR[k, v], WR[k, v]
            for a in (0, AZL - 1, *range(1, AZL - 1)):
                value = part[a]
                if a == 0:
                    value = value - HL[k, v]
                if a == AZL - 1:
                    value = value - HR[k, v]
                wall = jnp.where(is_outer, own[a][RC - 1 : RC], far[a : a + 1])
                at = base + a * ROWS
                top = value[0:8] - jnp.where(row == 0, outer * got[a : a + 1], 0.0)
                edge = value[40:48] - jnp.where(row == 7, share * got[a : a + 1], 0.0)
                skin = value[48:56] - jnp.where(row == 0, wet_rows[a] * wall, 0.0)
                X[k + 1, pl.ds(pl.multiple_of(at, 8), 8), :] = top
                X[k + 1, pl.ds(pl.multiple_of(at + 8, 8), 32), :] = value[8:40]
                X[k + 1, pl.ds(pl.multiple_of(at + 40, 8), 8), :] = edge
                X[k + 1, pl.ds(pl.multiple_of(at + 48, 8), 8), :] = skin
                if k + 1 < STEPS:
                    IS[k + 1, v, a : a + 1, :] = jnp.where(is_outer, top[0:1], edge[7:8])
                    WS[k + 1, v, a : a + 1, :] = edge[7:8]
                    if a == AZL - 1:
                        send_layers(k + 1, v)
            if k + 1 < STEPS:
                send_rest(k + 1, v)
            for hear, tell, when in (((None, 0, 0),), ((0, 1, 0), (1, 2, 5)), ((2, 3, 2),))[k]:

                @pl.when(v == when)
                def _(hear=hear, tell=tell):
                    if hear is not None:
                        hear_word(hear)
                    pass_word(tell)

            return products([(k, k, 16 * k), (k, k + 1, 16 * k + 8)], v, moments)

        return body

    def products(which, v, moments):
        k = which[0][0]
        base = v * BLK
        sums = [[jnp.zeros((8, 128), F32) for _ in range(NV)] for _ in which]
        for p in range(BLK // 8):
            here = pl.ds(pl.multiple_of(base + p * 8, 8), 8)
            mine = [X[j, here, :] for _, j, _ in which]
            if p % 7 == 6:
                mine = [m * share for m in mine]
            for w in range(NV):
                other = X[k, w * BLK + p * 8 : w * BLK + p * 8 + 8, :]
                for q in range(len(which)):
                    sums[q][w] += other * mine[q]
        for q, (_, _, at) in enumerate(which):
            for w in range(NV):
                ACC[64 * q + w * 8 : 64 * q + w * 8 + 8, :] = sums[q][w]
            total = ACC[pl.ds(64 * q, 8, stride=8), :]
            for s in range(1, 8):
                total += ACC[pl.ds(64 * q + s, 8, stride=8), :]
            total = jnp.sum(total, axis=1, keepdims=True)
            moments = jnp.where(lane == at + v, total, moments)
        return moments

    def sum_copy(stage, d):
        at = place_in(stage)
        return pltpu.make_async_remote_copy(
            RX.at[stage, at], RX.at[stage, at], sum_send.at[stage], sum_recv.at[stage],
            device_id=peer(stage, d)[1], device_id_type=MESH,
        )

    def sum_all(stage):
        n = slots[stage] - 1
        block = RX.at[stage, pl.ds(0, n)]
        return pltpu.make_async_remote_copy(
            block, block, sum_send.at[stage], sum_recv.at[stage],
            device_id=peer(stage, 1)[1], device_id_type=MESH,
        )

    def hops(stage, d):
        major, minor = d // 4, d % 4
        return min(minor, 4 - minor) + (min(major, 4 - major) if stage == 0 else 4 * major)

    def sum_start(stage, value):
        RX[stage, place_in(stage)] = value
        for d in sorted(range(1, slots[stage]), key=lambda d: hops(stage, d), reverse=True):
            sum_copy(stage, d).start()

    def sum_finish(stage):
        sum_all(stage).wait_recv()
        terms = [RX[stage, s] for s in range(slots[stage])]
        while len(terms) > 1:
            terms = [terms[q] + terms[q + 1] for q in range(0, len(terms), 2)]
        return terms[0]

    def prepare(r, c):
        for half in range(2):
            cols = [
                jnp.concatenate(
                    [X[k, pl.ds((2 * half + b) * ROWS + r, NV, stride=BLK), :] for k in range(4)], axis=0
                )
                for b in range(2)
            ]
            wide = jnp.concatenate(cols, axis=1)
            high = rounded(wide)
            T[2 * r + half] = jnp.concatenate([high, wide - high, high], axis=0).astype(BF16)
        return c

    zero8 = jnp.zeros((8, 128), F32)
    moments = zero8
    for k in range(STEPS):
        moments = lax.fori_loop(0, NV, apply(k), moments)
    sum_start(2, moments)
    hear_word(3)
    pl.semaphore_signal(word.at[4, 0], inc=1, device_id=to_half, device_id_type=MESH)
    sum_start(0, sum_finish(2))
    lax.fori_loop(0, 27, prepare, 0, unroll=3)
    for k in range(STEPS):
        sent(k)
    pl.semaphore_wait(word.at[4, 0], 1)
    sum_start(1, sum_finish(0))
    lax.fori_loop(27, 54, prepare, 0, unroll=3)
    for stage in (2, 0):
        sum_all(stage).wait_send()
    gram = sum_finish(1)

    shifted = pltpu.roll(gram, 120, axis=1) + THETA * gram
    table = []
    for i in range(STEPS):
        left_part = shifted if i == 0 else pltpu.roll(shifted, 128 - 8 * i, axis=1)
        right_part = pltpu.roll(gram, 24 - 8 * i, axis=1)
        table.append(jnp.where(lane < 24, left_part, jnp.where(lane < 32, right_part, 0.0)))
    full = (8, 128)

    def over(part):
        return jnp.broadcast_to(part, full)

    for at in range(STEPS):
        columns = [[over(t[:, 8 * at + q : 8 * at + q + 1]) for t in table] for q in range(8)]
        for r in range(8):
            inverse = 1.0 / over(columns[r][at][r : r + 1, :])
            scaled = over(table[at][r : r + 1, :]) * inverse
            ratios = {q: over(columns[q][at][r : r + 1, :]) * inverse for q in range(r + 1, 8)}
            for i in range(STEPS):
                for q, ratio in ratios.items():
                    reduced = columns[q][i] - columns[r][i] * ratio
                    columns[q][i] = jnp.where(row == r, ratio, reduced) if i == at else reduced
                reduced = table[i] - columns[r][i] * scaled
                table[i] = jnp.where(row == r, scaled, reduced) if i == at else reduced

    y = [jnp.where(lane < 8, pltpu.roll(t, 104, axis=1), 0.0) for t in table]
    eye = jnp.where(lane == row, 1.0, 0.0)
    into = [
        eye - THETA * y[0],
        -(y[0] + THETA * y[1]),
        -(y[1] + THETA * y[2]),
        -y[2],
    ]
    parts = [(y[k] if k < STEPS else zero8) + pltpu.roll(into[k], 8, axis=1) for k in range(4)]
    square = jnp.concatenate(parts, axis=0)
    turned = square.T[0:16, :]
    mix = jnp.concatenate([turned, jnp.zeros((16, 96), F32)], axis=1)
    high = rounded(mix)
    MIX[...] = high + pltpu.roll(high, 32, axis=1) + pltpu.roll(mix - high, 64, axis=1)
    sum_all(1).wait_send()


PIECES = 4


def finish_kernel(T, MIX, sol_c, res_c, sol_s, res_s, o_sc, o_rc, o_ss, o_rs, sem):
    mix = MIX[...].astype(BF16)[:, 0:96]

    def rows_of(first, rows, o_sol, o_res):
        def body(r, c):
            for a in (0, 2):
                out = jnp.dot(mix, T[2 * (first + r) + a // 2], preferred_element_type=F32)
                for b in range(2):
                    here = pl.ds(r * AZL + a + b, NV, stride=rows * AZL)
                    o_sol[here, :] = out[0:8, b * 128 : b * 128 + 128]
                    o_res[here, :] = out[8:16, b * 128 : b * 128 + 128]
            return c

        return body

    def piece(i, o, dst, slot, rows):
        copies = []
        for v in range(NV):
            here = pl.ds(v * RC * AZL + i * rows, rows)
            copies.append(pltpu.make_async_copy(o.at[here, :], dst.at[here, :], sem.at[slot]))
        return copies

    each = RC // PIECES
    lax.fori_loop(0, RS, rows_of(RC, RS, o_ss, o_rs), 0, unroll=True)
    small = [
        pltpu.make_async_copy(o_ss, sol_s, sem.at[2]),
        pltpu.make_async_copy(o_rs, res_s, sem.at[3]),
    ]
    for copy in small:
        copy.start()
    for i in range(PIECES):
        lax.fori_loop(i * each, (i + 1) * each, rows_of(0, RC, o_sc, o_rc), 0, unroll=True)
        for copy in piece(i, o_sc, sol_c, 0, each * AZL) + piece(i, o_rc, res_c, 1, each * AZL):
            copy.start()
    for copy in small:
        copy.wait()
    pltpu.make_async_copy(o_sc, sol_c, sem.at[0]).wait()
    pltpu.make_async_copy(o_rc, res_c, sem.at[1]).wait()


def per_device(cavity_block, shell_block, column_matrix, shell_matrix, shifted_diagonal, shell_diagonal, wet_area):
    nc, ns = NV * RC * AZL, NV * RS * AZL
    anywhere = pl.BlockSpec(memory_space=pl.ANY)
    args = (
        cavity_block.reshape(nc, 128),
        shell_block.reshape(ns, 128),
        column_matrix.reshape(RC, RC),
        shell_matrix,
        shifted_diagonal.reshape(RC * AZL, 128),
        shell_diagonal.reshape(RS * AZL, 128),
        wet_area,
    )
    args = [pltpu.with_memory_space_constraint(x, pltpu.HBM) for x in args]
    inside = pl.BlockSpec(memory_space=pltpu.VMEM)
    basis, mix = pl.pallas_call(
        kernel,
        out_shape=(pltpu.VMEM((2 * (RC + RS), 96, 256), BF16), pltpu.VMEM((16, 128), F32)),
        in_specs=[anywhere] * 7,
        out_specs=(inside, inside),
        scratch_shapes=[
            pltpu.VMEM((4, NV * BLK, 128), F32),
            pltpu.VMEM((STEPS, NV, ROWS, 128), F32),
            pltpu.VMEM((STEPS, NV, ROWS, 128), F32),
            pltpu.VMEM((STEPS, NV, BLK, 128), F32),
            pltpu.VMEM((STEPS, NV, AZL, 128), F32),
            pltpu.VMEM((STEPS, NV, AZL, 128), F32),
            pltpu.VMEM((STEPS, NV, AZL, 128), F32),
            pltpu.VMEM((STEPS, NV, AZL, 128), F32),
            pltpu.VMEM((AZL, ROWS, 128), F32),
            pltpu.VMEM((64, 256), BF16),
            pltpu.VMEM((64, 128), F32),
            pltpu.VMEM((128, 128), F32),
            pltpu.VMEM((3, 16, 8, 128), F32),
            pltpu.VMEM((nc, 128), F32),
            pltpu.VMEM((ns, 128), F32),
            pltpu.VMEM((RC * AZL, 128), F32),
            pltpu.VMEM((RS * AZL, 128), F32),
            pltpu.VMEM((AZL, 128), F32),
            pltpu.VMEM((RC, RC), F32),
            pltpu.VMEM((RS, RS), F32),
            pltpu.SemaphoreType.DMA((6,)),
            pltpu.SemaphoreType.DMA((NV,)),
            pltpu.SemaphoreType.DMA((STEPS, 5)),
            pltpu.SemaphoreType.DMA((STEPS, NV, 5)),
            pltpu.SemaphoreType.DMA((3,)),
            pltpu.SemaphoreType.DMA((3,)),
            pltpu.SemaphoreType.REGULAR((5, 2)),
        ],
        compiler_params=pltpu.CompilerParams(
            collective_id=0, has_side_effects=True, vmem_limit_bytes=22 * 1024 * 1024
        ),
        name="block_cg",
    )(*args)
    outs = pl.pallas_call(
        finish_kernel,
        out_shape=(
            jax.ShapeDtypeStruct((nc, 128), F32),
            jax.ShapeDtypeStruct((nc, 128), F32),
            jax.ShapeDtypeStruct((ns, 128), F32),
            jax.ShapeDtypeStruct((ns, 128), F32),
        ),
        in_specs=[inside, inside],
        out_specs=(anywhere,) * 4,
        scratch_shapes=[
            pltpu.VMEM((nc, 128), F32),
            pltpu.VMEM((nc, 128), F32),
            pltpu.VMEM((ns, 128), F32),
            pltpu.VMEM((ns, 128), F32),
            pltpu.SemaphoreType.DMA((4,)),
        ],
        compiler_params=pltpu.CompilerParams(vmem_limit_bytes=22 * 1024 * 1024),
        name="combine_basis",
    )(
        pltpu.with_memory_space_constraint(basis, pltpu.VMEM),
        pltpu.with_memory_space_constraint(mix, pltpu.VMEM),
    )
    return (
        outs[0].reshape(NV, RC, AZL, 128),
        outs[1].reshape(NV, RC, AZL, 128),
        outs[2].reshape(NV, RS, AZL, 128),
        outs[3].reshape(NV, RS, AZL, 128),
    )


def solution(mesh):
    return jax.shard_map(
        per_device,
        mesh=mesh,
        in_specs=(
            P(None, "grp", "az", "ax"),
            P(None, None, "az", "ax"),
            P("grp", None, None),
            P(),
            P("grp", "az", "ax"),
            P(None, "az", "ax"),
            P("az", "ax"),
        ),
        out_specs=(
            P(None, "grp", "az", "ax"),
            P(None, "grp", "az", "ax"),
            P(None, None, "az", "ax"),
            P(None, None, "az", "ax"),
        ),
        check_vma=False,
    )
```
